128 devices in a mesh: group: 8 (over y_hi, x), row: 16 (over z, y_lo, core).
Axes of the slice: x: 4, y: 4 (y_hi: 2, y_lo: 2; y = y_hi * 2 + y_lo), z: 4, core: 2. Of those that a mesh axis runs over, the one named last changes fastest.
Arguments:
- embeds: bfloat16 [65536, 768], P(('group', 'row')), may hold values from -120 to 120
- member: int32 [65536], P(('group', 'row')), may hold values from 0 to 7, as said below
Outputs:
- nearest: float32 [65536], P(('group', 'row'))
The draws below stay inside these ranges and needn't reach their ends.
Inputs may be any that keep to these rules, and one draw needn't show every extreme that they name: `member`: rows come in aligned blocks of 512; no cluster takes more than 128 rows of one block. For each remainder of the block index modulo the row axis's size, one cluster takes exactly 128 rows of every block with that remainder.
All inputs are finite; a program needn't handle non-finite values.
Results may differ from the reference program's by a relative error of at most 0.00056.
Values may be sent and summed in bfloat16 or wider, within the bound.
No kernel may reach another device: no remote copies, remote signals or barrier semaphores. Data moves between devices by JAX's collectives and lax.ppermute only.
A program may use at most 128 MiB of HBM per device.

```python
import math
import jax
import jax.numpy as jnp
from jax import lax

D = 768
RB = 512
ROWS = 65536
N_GROUP = 8
N_ROW = 16


def cluster_plan(key):
    per_cluster = 2 * RB // N_GROUP
    tickets = N_GROUP * per_cluster
    plan_key = jax.random.fold_in(key, 11)
    favour_key, block_key = jax.random.split(plan_key)
    favourite = jax.random.randint(favour_key, (N_ROW,), 0, N_GROUP)
    favourite_blocks = jnp.tile(favourite, N_GROUP)
    ticket_owner = jnp.arange(tickets, dtype=jnp.int32) // per_cluster

    def one_block(block_seed, chosen_cluster):
        order_key, shuffle_key = jax.random.split(block_seed)
        ranking_order = jax.random.permutation(order_key, tickets).astype(jnp.int32)
        priority = jnp.where(ticket_owner == chosen_cluster, jnp.arange(tickets, dtype=jnp.int32) - tickets, ranking_order)
        picked = ticket_owner[jnp.argsort(priority, stable=True)[:RB]]
        return picked[jax.random.permutation(shuffle_key, RB)]
    block_seeds = jax.random.split(block_key, N_GROUP * N_ROW)
    return jax.vmap(one_block)(block_seeds, favourite_blocks).reshape(-1).astype(jnp.int32)


def draw_member(key, part):
    membership = cluster_plan(key)
    return membership


def draw_embeds(key, part):
    membership = cluster_plan(key)
    key = jax.random.fold_in(key, 5)
    family_key, theme_key, weight_key, jitter_key, magnitude_key = jax.random.split(key, 5)
    families = max(RB * N_ROW // 4, 1)
    family = jax.random.randint(family_key, (ROWS,), 0, families)
    theme_number = membership * families + family

    def theme_vector(number):
        return jax.random.normal(jax.random.fold_in(theme_key, number), (D,))
    themes = jnp.clip(jax.vmap(theme_vector)(theme_number), -6.0, 6.0)
    mixing = jax.random.uniform(weight_key, (ROWS, 1), minval=0.2, maxval=0.95)
    jitter = jnp.clip(jax.random.normal(jitter_key, (ROWS, D)), -6.0, 6.0)
    magnitude = jnp.exp(jax.random.uniform(magnitude_key, (ROWS, 1), minval=0.0, maxval=math.log(10.0)))
    vectors = magnitude * (mixing * themes + jnp.sqrt(1.0 - mixing * mixing) * jitter)
    return vectors.astype(jnp.bfloat16)


def setup_inputs(seed: int = 0) -> dict:
    arg_keys = jax.random.split(jax.random.key(seed), 3)
    return {
        "embeds": draw_embeds(jax.random.fold_in(arg_keys[2], 71), 0),
        "member": draw_member(jax.random.fold_in(arg_keys[2], 71), 0),
    }


absent = -4.0

def reference(embeds, member):
    per_cluster = 2 * RB // N_GROUP
    slot_count = N_GROUP * per_cluster
    span = N_ROW * slot_count
    values = embeds.astype(jnp.float32)
    normed = (values * lax.rsqrt(lax.optimization_barrier(jnp.sum(values * values, axis=1, keepdims=True)) + 1e-06)).astype(jnp.bfloat16)
    blocks = member.reshape(N_GROUP * N_ROW, RB)
    hits = (blocks[:, :, None] == jnp.arange(N_GROUP, dtype=jnp.int32)[None, None, :]).astype(jnp.int32)
    ranking = lax.optimization_barrier(jnp.sum(jnp.cumsum(hits, axis=1) * hits, axis=2)) - 1
    block_index = jnp.arange(N_GROUP * N_ROW, dtype=jnp.int32)
    source = block_index // N_ROW
    along = block_index % N_ROW
    position = along[:, None] * slot_count + source[:, None] * per_cluster + ranking
    flat_index = (blocks * span + position).reshape(-1).astype(jnp.int32)
    table = jnp.zeros((N_GROUP * span, D), jnp.bfloat16).at[flat_index].set(normed)
    filled = jnp.zeros((N_GROUP * span,), jnp.bool_).at[flat_index].set(True)
    table = table.reshape(N_GROUP, span, D)
    filled = filled.reshape(N_GROUP, span)
    every_slot = jnp.arange(span, dtype=jnp.int32)

    def one_cluster(pair):
        cluster_rows, cluster_filled = pair

        def one_block(block_number):
            own_rows = lax.dynamic_slice_in_dim(cluster_rows, block_number * slot_count, slot_count, 0)
            scores = jnp.dot(own_rows, cluster_rows.T, preferred_element_type=jnp.float32)
            own_ids = block_number * slot_count + jnp.arange(slot_count, dtype=jnp.int32)
            keep = cluster_filled[None, :] & (own_ids[:, None] != every_slot[None, :])
            return lax.optimization_barrier(jnp.max(jnp.where(keep, scores, absent), axis=1))
        return lax.map(one_block, jnp.arange(N_ROW, dtype=jnp.int32)).reshape(-1)
    best_slots = lax.map(one_cluster, (table, filled)).reshape(-1)
    return best_slots[flat_index]
```

```python
import functools

import jax
import jax.numpy as jnp
from jax import lax
from jax.experimental import pallas as pl
from jax.experimental.pallas import tpu as pltpu
from jax.sharding import PartitionSpec as P

D = 768
RB = 512
GROUPS = 8
MOST = 128
META = 16
SENT = RB + META
HELD = 640
SHORT, LONG = 80, 144
TILE = 256
ABSENT = -4.0
LOW = -1e30
AXES = ("group", "row")

UNIT = ((1, 0, 0), (0, 1, 0), (0, 0, 1), (3, 0, 0), (0, 3, 0), (0, 0, 3))
PARENT = (None,) + (0, 0, 0, 2, 3, 1, 4, 5, 5, 6, 6, 4)
DIRS = (
    (None,) + (0, 1, 3, 5, 2, 4, 3, 4, 1, 0, 5, 1),
    (None,) + (2, 5, 4, 1, 0, 3, 0, 2, 5, 2, 4, 3),
)
SLOTS = len(PARENT)
FLIPPED = 10


def offsets():
    table = []
    for core in range(2):
        held = [(0, 0, 0)]
        for i in range(1, SLOTS):
            step, base = UNIT[DIRS[core][i]], held[PARENT[i]]
            held.append(tuple((a + b) % 4 for a, b in zip(step, base)))
        table.append(held)
    return table


def place(x, y, z, core):
    group = (y // 2) * 4 + x
    row = (z * 2 + y % 2) * 2 + core
    return group * 16 + row


def fetch(block, steps):
    pairs = []
    for x in range(4):
        for y in range(4):
            for z in range(4):
                for core in range(2):
                    dx, dy, dz = steps[core]
                    source = place((x + dx) % 4, (y + dy) % 4, (z + dz) % 4, core)
                    pairs.append((source, place(x, y, z, core)))
    return lax.ppermute(block, AXES, sorted(pairs))


def flip(block):
    return lax.ppermute(block, AXES, [(i, i ^ 1) for i in range(128)])


def prepare_kernel(embeds_ref, member_ref, block_ref, target_ref):
    member = member_ref[...].astype(jnp.float32)
    column = jnp.transpose(jnp.broadcast_to(member, (128, RB)))[:, 0:1]
    above = lax.broadcasted_iota(jnp.int32, (RB, RB), 0)
    across = lax.broadcasted_iota(jnp.int32, (RB, RB), 1)
    before = (column < member) | ((column == member) & (above < across))
    target = jnp.sum(before.astype(jnp.float32), axis=0, keepdims=True).astype(jnp.int32)
    target_ref[...] = target
    values = embeds_ref[...].astype(jnp.float32)
    total = jnp.sum(values * values, axis=1, keepdims=True)
    normed = (values * lax.rsqrt(total + 1e-06)).astype(jnp.bfloat16)
    placer = (above == target).astype(jnp.bfloat16)
    block_ref[0:RB, :] = jnp.dot(placer, normed, preferred_element_type=jnp.float32).astype(
        jnp.bfloat16
    )
    lane = lax.broadcasted_iota(jnp.int32, (RB, D), 1).astype(jnp.float32)
    counts = jnp.sum((column == lane).astype(jnp.float32), axis=0, keepdims=True)
    block_ref[RB:SENT, :] = jnp.broadcast_to(counts, (META, D)).astype(jnp.bfloat16)


def prepare(embeds, member):
    return pl.pallas_call(
        prepare_kernel,
        out_shape=(
            jax.ShapeDtypeStruct((SENT, D), jnp.bfloat16),
            jax.ShapeDtypeStruct((1, RB), jnp.int32),
        ),
        name="prepare",
    )(embeds, member.reshape(1, RB))


def gram_kernel(new, total, *refs):
    blocks = refs[:total]
    out_ref = refs[total]
    (held, rows, bias, best, kept, counts_v, counts_s, start_s, put_s, sems, meta_sem) = refs[
        total + 1 :
    ]
    copies = []
    for k in range(total):
        copy = pltpu.make_async_copy(blocks[k], held.at[k, pl.ds(0, SENT)], sems.at[k])
        copy.start()
        copies.append(copy)
    rows[...] = jnp.zeros_like(rows)
    for k in range(total):
        held[k, SENT:HELD, :] = jnp.zeros((HELD - SENT, D), jnp.bfloat16)
        kept[k] = jnp.full((HELD, 128), LOW, jnp.float32)
        start_s[k] = 0
    for k in range(total):
        copies[k].wait()
        counts_v[k : k + 1, :] = held[k, RB:SENT, 0:128].astype(jnp.float32)[0:1].astype(jnp.int32)
    fetch_counts = pltpu.make_async_copy(counts_v, counts_s, meta_sem)
    fetch_counts.start()
    fetch_counts.wait()

    def bias_of(length, first, low, high):
        at = first + lax.broadcasted_iota(jnp.int32, (length, 128), 0)
        return jnp.where((at >= low) & (at < high), 0.0, LOW)

    def one_cluster(c, carry):
        put = jnp.int32(0)
        new_rows = jnp.int32(0)
        for k in range(total):
            low = start_s[k]
            high = low + counts_s[k, c]
            first = pl.multiple_of((low // 16) * 16, 16)
            tiles = jnp.where(high > low, (high - first + 15) // 16, 0)
            put = pl.multiple_of(put, 16)
            put_s[k] = put

            @pl.when(tiles > 0)
            def _(k=k, low=low, high=high, first=first, put=put):
                rows[pl.ds(put, SHORT), :] = held[k, pl.ds(first, SHORT), :]
                bias[pl.ds(put, SHORT), :] = bias_of(SHORT, first, low, high)

            @pl.when(tiles > SHORT // 16)
            def _(k=k, low=low, high=high, first=first, put=put):
                more = pl.multiple_of(put + SHORT, 16)
                rest = pl.multiple_of(first + SHORT, 16)
                rows[pl.ds(more, LONG - SHORT), :] = held[k, pl.ds(rest, LONG - SHORT), :]
                bias[pl.ds(more, LONG - SHORT), :] = bias_of(LONG - SHORT, rest, low, high)

            put = put + tiles * 16
            if k == new - 1:
                new_rows = put
        put = pl.multiple_of(put, 16)
        bias[pl.ds(put, TILE), :] = jnp.full((TILE, 128), LOW, jnp.float32)
        column_tiles = (new_rows + TILE - 1) // TILE
        row_tiles = (put + TILE - 1) // TILE

        def clear(m, carry):
            best[pl.ds(pl.multiple_of(m * TILE, TILE), TILE), :] = jnp.full(
                (TILE, 128), LOW, jnp.float32
            )
            return carry

        lax.fori_loop(0, row_tiles, clear, 0)

        def one_column_tile(n, carry):
            here = pl.multiple_of(n * TILE, TILE)
            columns = rows[pl.ds(here, TILE), :]
            column_bias = jnp.transpose(bias[pl.ds(here, TILE), :])[0:1, :]

            def visit(scores, at, column_best):
                masked = scores + column_bias
                best[pl.ds(at, TILE), :] = jnp.maximum(
                    best[pl.ds(at, TILE), :],
                    jnp.maximum(masked[:, :128], masked[:, 128:]),
                )
                row_bias = bias[pl.ds(at, TILE), :]
                masked = scores + jnp.concatenate([row_bias, row_bias], axis=1)
                return jnp.maximum(column_best, jnp.max(masked.reshape(TILE // 8, 8, TILE), axis=0))

            def scores_at(at):
                return lax.dot_general(
                    rows[pl.ds(at, TILE), :],
                    columns,
                    (((1,), (1,)), ((), ())),
                    preferred_element_type=jnp.float32,
                )

            same = lax.broadcasted_iota(jnp.int32, (TILE, TILE), 0) == lax.broadcasted_iota(
                jnp.int32, (TILE, TILE), 1
            )
            column_best = jnp.full((8, TILE), LOW, jnp.float32)
            column_best = visit(jnp.where(same, LOW, scores_at(here)), here, column_best)

            def one_row_tile(m, column_best):
                at = pl.multiple_of(m * TILE, TILE)
                return visit(scores_at(at), at, column_best)

            column_best = lax.fori_loop(n + 1, row_tiles, one_row_tile, column_best)
            top = jnp.max(column_best, axis=0, keepdims=True)
            down = jnp.transpose(jnp.broadcast_to(top, (128, TILE)))
            best[pl.ds(here, TILE), :] = jnp.maximum(best[pl.ds(here, TILE), :], down)
            return carry

        lax.fori_loop(0, column_tiles, one_column_tile, 0)

        for k in range(total):
            low = start_s[k]
            high = low + counts_s[k, c]
            first = pl.multiple_of((low // 16) * 16, 16)
            tiles = jnp.where(high > low, (high - first + 15) // 16, 0)
            put = pl.multiple_of(put_s[k], 16)

            def keep(k, first, put, length):
                kept[k, pl.ds(first, length), :] = jnp.maximum(
                    kept[k, pl.ds(first, length), :],
                    best[pl.ds(put, length), :] + bias_of(length, first, low, high),
                )

            @pl.when(tiles > 0)
            def _(k=k, low=low, high=high, first=first, put=put):
                kept[k, pl.ds(first, SHORT), :] = jnp.maximum(
                    kept[k, pl.ds(first, SHORT), :],
                    best[pl.ds(put, SHORT), :] + bias_of(SHORT, first, low, high),
                )

            @pl.when(tiles > SHORT // 16)
            def _(k=k, low=low, high=high, first=first, put=put):
                more = pl.multiple_of(put + SHORT, 16)
                rest = pl.multiple_of(first + SHORT, 16)
                kept[k, pl.ds(rest, LONG - SHORT), :] = jnp.maximum(
                    kept[k, pl.ds(rest, LONG - SHORT), :],
                    best[pl.ds(more, LONG - SHORT), :] + bias_of(LONG - SHORT, rest, low, high),
                )

            start_s[k] = high
        return carry

    lax.fori_loop(0, GROUPS, one_cluster, 0)
    for k in range(total):
        turned = jnp.transpose(kept[k, 0:RB, :])
        out_ref[k : k + 1, :] = jnp.max(turned, axis=0, keepdims=True)


def gram(new_blocks, old_blocks):
    new, total = len(new_blocks), len(new_blocks) + len(old_blocks)
    deep = -(-(total * LONG) // TILE) * TILE + TILE
    return pl.pallas_call(
        functools.partial(gram_kernel, new, total),
        out_shape=jax.ShapeDtypeStruct((total, RB), jnp.float32),
        in_specs=[pl.BlockSpec(memory_space=pl.ANY)] * total,
        scratch_shapes=[
            pltpu.VMEM((total, HELD, D), jnp.bfloat16),
            pltpu.VMEM((deep, D), jnp.bfloat16),
            pltpu.VMEM((deep, 128), jnp.float32),
            pltpu.VMEM((deep, 128), jnp.float32),
            pltpu.VMEM((total, HELD, 128), jnp.float32),
            pltpu.VMEM((total, 128), jnp.int32),
            pltpu.SMEM((total, 128), jnp.int32),
            pltpu.SMEM((total,), jnp.int32),
            pltpu.SMEM((total,), jnp.int32),
            pltpu.SemaphoreType.DMA((total,)),
            pltpu.SemaphoreType.DMA,
        ],
        compiler_params=pltpu.CompilerParams(vmem_limit_bytes=56 * 2**20),
        cost_estimate=pl.CostEstimate(
            flops=2 * 8 * 70 * 70 * D * new * total, bytes_accessed=total * SENT * D * 2, transcendentals=0
        ),
        name=f"gram_{new}_{total}",
    )(*new_blocks, *old_blocks)


def scatter_kernel(found_ref, where_ref, out_ref):
    out_ref[...] = jnp.full_like(out_ref, ABSENT)
    for k in range(found_ref.shape[0]):
        out_ref[pl.ds(where_ref[k], 1), :] = jnp.maximum(found_ref[k : k + 1, :], ABSENT)


def scatter(found, where):
    return pl.pallas_call(
        scatter_kernel,
        out_shape=jax.ShapeDtypeStruct((128, RB), jnp.float32),
        in_specs=[pl.BlockSpec(memory_space=pltpu.VMEM), pl.BlockSpec(memory_space=pltpu.SMEM)],
        out_specs=pl.BlockSpec(memory_space=pltpu.VMEM),
        name="scatter",
    )(found, where)


def finish_kernel(arrived_ref, target_ref, out_ref):
    best = jnp.max(arrived_ref[...], axis=0, keepdims=True)
    column = jnp.transpose(jnp.broadcast_to(best, (128, RB)))[:, 0:1]
    above = lax.broadcasted_iota(jnp.int32, (RB, RB), 0)
    picked = jnp.where(above == target_ref[...], column, LOW)
    out_ref[...] = jnp.max(picked, axis=0, keepdims=True)


def finish(arrived, target):
    return pl.pallas_call(
        finish_kernel, out_shape=jax.ShapeDtypeStruct((1, RB), jnp.float32), name="finish"
    )(arrived, target)


def homes():
    group, row = lax.axis_index("group"), lax.axis_index("row")
    x, y, z, core = group % 4, (group // 4) * 2 + (row // 2) % 2, row // 4, row % 2
    table = jnp.array(offsets(), jnp.int32)
    own = jnp.where(core == 0, table[0], table[1])
    other = jnp.where(core == 0, table[1], table[0])[:FLIPPED]
    cores = jnp.concatenate([jnp.full((SLOTS,), core), jnp.full((FLIPPED,), 1 - core)])
    steps = jnp.concatenate([own, other])
    return place((x + steps[:, 0]) % 4, (y + steps[:, 1]) % 4, (z + steps[:, 2]) % 4, cores).astype(
        jnp.int32
    )


def on_device(embeds, member):
    block, target = prepare(embeds, member)
    held = [block]
    for i in range(1, SLOTS):
        held.append(fetch(held[PARENT[i]], (UNIT[DIRS[0][i]], UNIT[DIRS[1][i]])))
    flipped = [flip(held[i]) for i in range(FLIPPED)]
    found = gram(held, flipped)
    outgoing = scatter(found, homes())
    arrived = lax.all_to_all(outgoing, AXES, split_axis=0, concat_axis=0, tiled=True)
    return finish(arrived, target).reshape(-1)


def solution(mesh):
    in_specs = (P(AXES, None), P(AXES))
    return jax.shard_map(
        on_device, mesh=mesh, in_specs=in_specs, out_specs=P(AXES), check_vma=False
    )
```

```python
import functools

import jax
import jax.numpy as jnp
import numpy as np
from jax import lax
from jax.experimental import pallas as pl
from jax.experimental.pallas import tpu as pltpu
from jax.sharding import PartitionSpec as P

D = 768
RB = 512
GROUPS = 8
META = 16
SENT = RB + META
HELD = 640
SHORT, LONG = 80, 144
TILE = 256
STRIP = 512
ABSENT = -4.0
LOW = -1e30
AXES = ("group", "row")

UNIT = ((1, 0, 0), (0, 1, 0), (0, 0, 1), (3, 0, 0), (0, 3, 0), (0, 0, 3))
PARENT = (None,) + (0, 0, 0, 1, 2, 0, 5, 4, 1, 8, 9, 6)
DIRS = (
    (None,) + (5, 3, 2, 1, 4, 0, 4, 3, 5, 5, 0, 2),
    (None,) + (1, 0, 4, 5, 2, 3, 2, 0, 1, 1, 3, 4),
)
SLOTS = len(PARENT)
OTHER = 20
MEETINGS = (
    ((0, 3, 23), (1, 2), True),
    ((4, 5, 6), (0, 2, 3, 20, 21, 22, 23, 25, 26), True),
    ((7, 8, 9), (0, 1, 2, 3, 4, 5, 6, 22, 24, 25, 26, 27, 29), True),
    ((10, 11, 12), (2, 5, 7, 23, 24, 26, 29), False),
)
NAMES = tuple(sorted({k for meeting in MEETINGS for k in meeting[0] + meeting[1]}))


def offsets():
    table = []
    for core in range(2):
        held = [(0, 0, 0)]
        for i in range(1, SLOTS):
            step, base = UNIT[DIRS[core][i]], held[PARENT[i]]
            held.append(tuple((a + b) % 4 for a, b in zip(step, base)))
        table.append(held)
    return table


def place(x, y, z, core):
    group = (y // 2) * 4 + x
    row = (z * 2 + y % 2) * 2 + core
    return group * 16 + row


def fetch(block, steps):
    pairs = []
    for x in range(4):
        for y in range(4):
            for z in range(4):
                for core in range(2):
                    dx, dy, dz = steps[core]
                    source = place((x + dx) % 4, (y + dy) % 4, (z + dz) % 4, core)
                    pairs.append((source, place(x, y, z, core)))
    return lax.ppermute(block, AXES, sorted(pairs))


def flip(block):
    return lax.ppermute(block, AXES, [(i, i ^ 1) for i in range(128)])


def prepare_kernel(embeds_ref, member_ref, block_ref, target_ref):
    member = member_ref[...].astype(jnp.float32)
    column = jnp.transpose(jnp.broadcast_to(member, (128, RB)))[:, 0:1]
    above = lax.broadcasted_iota(jnp.int32, (RB, RB), 0)
    across = lax.broadcasted_iota(jnp.int32, (RB, RB), 1)
    before = (column < member) | ((column == member) & (above < across))
    target = jnp.sum(before.astype(jnp.float32), axis=0, keepdims=True).astype(jnp.int32)
    target_ref[...] = target
    values = embeds_ref[...].astype(jnp.float32)
    total = jnp.sum(values * values, axis=1, keepdims=True)
    normed = (values * lax.rsqrt(total + 1e-06)).astype(jnp.bfloat16)
    placer = (above == target).astype(jnp.bfloat16)
    block_ref[0:RB, :] = jnp.dot(placer, normed, preferred_element_type=jnp.float32).astype(
        jnp.bfloat16
    )
    lane = lax.broadcasted_iota(jnp.int32, (RB, D), 1).astype(jnp.float32)
    counts = jnp.sum((column == lane).astype(jnp.float32), axis=0, keepdims=True)
    block_ref[RB:SENT, :] = jnp.broadcast_to(counts, (META, D)).astype(jnp.bfloat16)


def prepare(embeds, member):
    return pl.pallas_call(
        prepare_kernel,
        out_shape=(
            jax.ShapeDtypeStruct((SENT, D), jnp.bfloat16),
            jax.ShapeDtypeStruct((1, RB), jnp.int32),
        ),
        name="prepare",
    )(embeds, member.reshape(1, RB))


def gram_kernel(new, total, among, lists, *refs):
    blocks, refs = refs[:total], refs[total:]
    if lists:
        where_ref, refs = refs[0], refs[1:]
        before, refs = refs[: len(lists) - 1], refs[len(lists) - 1 :]
    out_ref, refs = refs[0], refs[1:]
    (held, rows, bias, best, kept, turned, counts_v, counts_s, start_s, put_s, sems, meta_sem) = (
        refs
    )
    copies = []
    for k in range(total):
        copy = pltpu.make_async_copy(blocks[k], held.at[k, pl.ds(0, SENT)], sems.at[k])
        copy.start()
        copies.append(copy)
    rows[...] = jnp.zeros_like(rows)
    for k in range(total):
        held[k, SENT:HELD, :] = jnp.zeros((HELD - SENT, D), jnp.bfloat16)
        kept[k] = jnp.full((HELD, 128), LOW, jnp.float32)
        start_s[k] = 0
    for k in range(total):
        copies[k].wait()
        counts_v[k : k + 1, :] = held[k, RB:SENT, 0:128].astype(jnp.float32)[0:1].astype(jnp.int32)
    fetch_counts = pltpu.make_async_copy(counts_v, counts_s, meta_sem)
    fetch_counts.start()
    fetch_counts.wait()

    def segment(k, c):
        low = start_s[k]
        high = low + counts_s[k, c]
        first = pl.multiple_of((low // 16) * 16, 16)
        tiles = jnp.where(high > low, (high - first + 15) // 16, 0)
        return low, high, first, tiles

    def bias_of(length, first, low, high):
        at = first + lax.broadcasted_iota(jnp.int32, (length, 128), 0)
        return jnp.where((at >= low) & (at < high), 0.0, LOW)

    def one_cluster(c, carry):
        put = jnp.int32(0)
        new_rows = put
        for k in range(total):
            low, high, first, tiles = segment(k, c)
            put = pl.multiple_of(put, 16)
            put_s[k] = put

            def gather(skip, length, k=k, low=low, high=high, first=first, put=put):
                source = pl.multiple_of(first + skip, 16)
                at = pl.multiple_of(put + skip, 16)
                rows[pl.ds(at, length), :] = held[k, pl.ds(source, length), :]
                bias[pl.ds(at, length), :] = bias_of(length, source, low, high)

            pl.when(tiles > 0)(functools.partial(gather, 0, SHORT))
            pl.when(tiles > SHORT // 16)(functools.partial(gather, SHORT, LONG - SHORT))
            put = put + tiles * 16
            if k == new - 1:
                new_rows = put
        put = pl.multiple_of(put, 16)
        bias[pl.ds(put, STRIP), :] = jnp.full((STRIP, 128), LOW, jnp.float32)

        def clear(m, carry):
            at = pl.multiple_of(m * TILE, TILE)
            best[pl.ds(at, TILE), :] = jnp.full((TILE, 128), LOW, jnp.float32)
            return carry

        lax.fori_loop(0, (put + STRIP + TILE - 1) // TILE, clear, 0)

        def one_column_tile(n, carry):
            here = pl.multiple_of(n * TILE, TILE)
            turned[...] = jnp.transpose(rows[pl.ds(here, TILE), :])
            inside = here + lax.broadcasted_iota(jnp.int32, (1, TILE), 1) < new_rows
            column_bias = jnp.transpose(bias[pl.ds(here, TILE), :])[0:1, :]
            column_bias = jnp.where(inside, column_bias, LOW)

            def visit(at, length, diagonal, column_best):
                scores = jnp.dot(
                    rows[pl.ds(at, length), :], turned[...], preferred_element_type=jnp.float32
                )
                if diagonal:
                    same = lax.broadcasted_iota(jnp.int32, (TILE, TILE), 0)
                    same = same == lax.broadcasted_iota(jnp.int32, (TILE, TILE), 1)
                    scores = jnp.where(same, LOW, scores)
                masked = scores + column_bias
                best[pl.ds(at, length), :] = jnp.maximum(
                    best[pl.ds(at, length), :],
                    jnp.maximum(masked[:, :128], masked[:, 128:]),
                )
                row_bias = bias[pl.ds(at, length), :]
                masked = scores + jnp.concatenate([row_bias, row_bias], axis=1)
                top = jnp.max(masked.reshape(length // 8, 8, TILE), axis=0)
                return jnp.maximum(column_best, top)

            column_best = jnp.full((8, TILE), LOW, jnp.float32)
            if among:
                column_best = visit(here, TILE, True, column_best)
                rest = pl.multiple_of(here + TILE, 16)
            else:
                rest = pl.multiple_of(new_rows, 16)

            def strip(i, column_best):
                at = pl.multiple_of(rest + i * STRIP, 16)
                return visit(at, STRIP, False, column_best)

            strips = jnp.maximum(put - rest + STRIP - 1, 0) // STRIP
            column_best = lax.fori_loop(0, strips, strip, column_best)
            top = jnp.where(inside, jnp.max(column_best, axis=0, keepdims=True), LOW)
            down = jnp.transpose(jnp.broadcast_to(top, (128, TILE)))
            best[pl.ds(here, TILE), :] = jnp.maximum(best[pl.ds(here, TILE), :], down)
            return carry

        lax.fori_loop(0, (new_rows + TILE - 1) // TILE, one_column_tile, 0)

        for k in range(total):
            low, high, first, tiles = segment(k, c)
            put = pl.multiple_of(put_s[k], 16)

            def keep(skip, length, k=k, low=low, high=high, first=first, put=put):
                at = pl.multiple_of(first + skip, 16)
                source = pl.multiple_of(put + skip, 16)
                fresh = best[pl.ds(source, length), :] + bias_of(length, at, low, high)
                kept[k, pl.ds(at, length), :] = jnp.maximum(kept[k, pl.ds(at, length), :], fresh)

            pl.when(tiles > 0)(functools.partial(keep, 0, SHORT))
            pl.when(tiles > SHORT // 16)(functools.partial(keep, SHORT, LONG - SHORT))
            start_s[k] = high
        return carry

    lax.fori_loop(0, GROUPS, one_cluster, 0)

    def found_in(k):
        return jnp.max(jnp.transpose(kept[k, 0:RB, :]), axis=0, keepdims=True)

    if not lists:
        for k in range(total):
            out_ref[k : k + 1, :] = found_in(k)
        return
    out_ref[...] = jnp.full_like(out_ref, ABSENT)
    for number, name in enumerate(NAMES):
        found = jnp.full((1, RB), ABSENT, jnp.float32)
        if name in lists[0]:
            found = jnp.maximum(found, found_in(lists[0].index(name)))
        for ref, names in zip(before, lists[1:]):
            if name in names:
                at = names.index(name)
                found = jnp.maximum(found, ref[at : at + 1, :])
        out_ref[where_ref[number]] = found


def gram(blocks, new, among, lists=(), where=None, before=()):
    total = len(blocks)
    deep = -(-(total * LONG) // TILE) * TILE + 2 * STRIP
    shape = (128, 1, RB) if lists else (total, RB)
    in_specs = [pl.BlockSpec(memory_space=pl.ANY)] * total
    if lists:
        in_specs += [pl.BlockSpec(memory_space=pltpu.SMEM)]
        in_specs += [pl.BlockSpec(memory_space=pltpu.VMEM)] * len(before)
    return pl.pallas_call(
        functools.partial(gram_kernel, new, total, among, lists),
        out_shape=jax.ShapeDtypeStruct(shape, jnp.float32),
        in_specs=in_specs,
        scratch_shapes=[
            pltpu.VMEM((total, HELD, D), jnp.bfloat16),
            pltpu.VMEM((deep, D), jnp.bfloat16),
            pltpu.VMEM((deep, 128), jnp.float32),
            pltpu.VMEM((deep, 128), jnp.float32),
            pltpu.VMEM((total, HELD, 128), jnp.float32),
            pltpu.VMEM((D, TILE), jnp.bfloat16),
            pltpu.VMEM((total, 128), jnp.int32),
            pltpu.SMEM((total, 128), jnp.int32),
            pltpu.SMEM((total,), jnp.int32),
            pltpu.SMEM((total,), jnp.int32),
            pltpu.SemaphoreType.DMA((total,)),
            pltpu.SemaphoreType.DMA,
        ],
        compiler_params=pltpu.CompilerParams(vmem_limit_bytes=48 * 2**20),
        cost_estimate=pl.CostEstimate(
            flops=2 * GROUPS * 160 * 160 * D * new * total,
            bytes_accessed=total * SENT * D * 2,
            transcendentals=0,
        ),
        name=f"gram_{new}_{total}",
    )(*blocks, *(() if where is None else (where,)), *before)


def finish_kernel(arrived_ref, target_ref, out_ref):
    best = jnp.max(arrived_ref[...], axis=0, keepdims=True)
    column = jnp.transpose(jnp.broadcast_to(best, (128, RB)))[:, 0:1]
    above = lax.broadcasted_iota(jnp.int32, (RB, RB), 0)
    picked = jnp.where(above == target_ref[...], column, LOW)
    out_ref[...] = jnp.max(picked, axis=0, keepdims=True)


def finish(arrived, target):
    return pl.pallas_call(
        finish_kernel, out_shape=jax.ShapeDtypeStruct((1, RB), jnp.float32), name="finish"
    )(arrived, target)


def homes():
    group, row = lax.axis_index("group"), lax.axis_index("row")
    x, y, z, core = group % 4, (group // 4) * 2 + (row // 2) % 2, row // 4, row % 2
    table = jnp.array(offsets(), jnp.int32)
    own = jnp.where(core == 0, table[0], table[1])
    other = jnp.where(core == 0, table[1], table[0])
    names = np.array(NAMES)
    steps = jnp.where((names < OTHER)[:, None], own[names % OTHER], other[names % OTHER])
    cores = jnp.where(names < OTHER, core, 1 - core)
    at = place((x + steps[:, 0]) % 4, (y + steps[:, 1]) % 4, (z + steps[:, 2]) % 4, cores)
    return at.astype(jnp.int32)


def on_device(embeds, member):
    block, target = prepare(embeds, member)
    held = {0: block}
    for i in range(1, SLOTS):
        held[i] = fetch(held[PARENT[i]], (UNIT[DIRS[0][i]], UNIT[DIRS[1][i]]))
    for name in NAMES:
        if name >= OTHER:
            held[name] = flip(held[name - OTHER])
    before, lists = [], []
    for columns, beside, among in MEETINGS[:-1]:
        names = columns + beside
        before.append(gram([held[k] for k in names], len(columns), among))
        lists.append(names)
    columns, beside, among = MEETINGS[-1]
    lists = [columns + beside] + lists
    outgoing = gram(
        [held[k] for k in lists[0]], len(columns), among, tuple(lists), homes(), tuple(before)
    )
    arrived = lax.all_to_all(outgoing, AXES, split_axis=0, concat_axis=0, tiled=True)
    return finish(arrived.reshape(128, RB), target).reshape(-1)


def solution(mesh):
    in_specs = (P(AXES, None), P(AXES))
    return jax.shard_map(
        on_device, mesh=mesh, in_specs=in_specs, out_specs=P(AXES), check_vma=False
    )
```

```python
import functools

import jax
import jax.numpy as jnp
import numpy as np
from jax import lax
from jax.experimental import pallas as pl
from jax.experimental.pallas import tpu as pltpu
from jax.sharding import PartitionSpec as P

D = 768
RB = 512
GROUPS = 8
META = 16
SENT = RB + META
UNROLL = 4
ABSENT = -4.0
LOW = -1e30
AXES = ("group", "row")

UNIT = ((1, 0, 0), (0, 1, 0), (0, 0, 1), (3, 0, 0), (0, 3, 0), (0, 0, 3))
PARENT = (None,) + (0, 0, 0, 2, 1, 3, 6, 4, 4, 5, 5, 7)
DIRS = (
    (None,) + (5, 0, 2, 1, 3, 4, 0, 5, 1, 5, 2, 0),
    (None,) + (4, 3, 1, 2, 0, 5, 3, 4, 2, 4, 1, 3),
)
SLOTS = len(PARENT)
OTHER = 20
MEETINGS = (
    ((0, (0, 20)), (1, (0, 20, 21)), (2, (0, 1, 20, 21)), (3, (1, 2, 20, 21))),
    (
        (4, (0, 1, 2, 3, 21, 22)),
        (5, (2, 3, 4, 20, 21, 23, 24, 25)),
        (6, (0, 1, 4, 5, 20, 22, 23, 25, 26)),
    ),
    (
        (7, (0, 3, 4, 5, 21, 22, 23, 24, 26, 27)),
        (8, (3, 5, 6, 7, 20, 21, 24, 25, 27)),
        (9, (0, 1, 2, 5, 6, 8, 22, 26, 27)),
    ),
    ((10, (2, 9, 20, 21, 23)), (11, (2, 8, 9, 20, 26)), (12, (23, 27))),
)


def members(meeting):
    rows = tuple(k for k, partners in meeting)
    rest = sorted({k for row, partners in meeting for k in partners} - set(rows))
    return rows, rows + tuple(rest)


NAMES = tuple(sorted({k for meeting in MEETINGS for k in members(meeting)[1]}))


def offsets():
    table = []
    for core in range(2):
        held = [(0, 0, 0)]
        for i in range(1, SLOTS):
            step, base = UNIT[DIRS[core][i]], held[PARENT[i]]
            held.append(tuple((a + b) % 4 for a, b in zip(step, base)))
        table.append(held)
    return table


def place(x, y, z, core):
    group = (y // 2) * 4 + x
    row = (z * 2 + y % 2) * 2 + core
    return group * 16 + row


def fetch(block, steps):
    pairs = []
    for x in range(4):
        for y in range(4):
            for z in range(4):
                for core in range(2):
                    dx, dy, dz = steps[core]
                    source = place((x + dx) % 4, (y + dy) % 4, (z + dz) % 4, core)
                    pairs.append((source, place(x, y, z, core)))
    return lax.ppermute(block, AXES, sorted(pairs))


def flip(block):
    return lax.ppermute(block, AXES, [(i, i ^ 1) for i in range(128)])


def prepare_kernel(embeds_ref, member_ref, block_ref, target_ref):
    member = member_ref[...].astype(jnp.float32)
    column = jnp.transpose(jnp.broadcast_to(member, (128, RB)))[:, 0:1]
    above = lax.broadcasted_iota(jnp.int32, (RB, RB), 0)
    across = lax.broadcasted_iota(jnp.int32, (RB, RB), 1)
    before = (column < member) | ((column == member) & (above < across))
    target = jnp.sum(before.astype(jnp.float32), axis=0, keepdims=True).astype(jnp.int32)
    target_ref[...] = target
    values = embeds_ref[...].astype(jnp.float32)
    total = jnp.sum(values * values, axis=1, keepdims=True)
    normed = (values * lax.rsqrt(total + 1e-06)).astype(jnp.bfloat16)
    placer = (above == target).astype(jnp.bfloat16)
    block_ref[0:RB, :] = jnp.dot(placer, normed, preferred_element_type=jnp.float32).astype(
        jnp.bfloat16
    )
    ordered = jnp.sum(jnp.where(above == target, member, 0.0), axis=1, keepdims=True)
    ordered = jnp.transpose(jnp.broadcast_to(ordered, (RB, 128)))[0:META]
    block_ref[RB:SENT, :] = jnp.zeros((META, D), jnp.bfloat16)
    block_ref[RB:SENT, 0:RB] = ordered.astype(jnp.bfloat16)


def prepare(embeds, member):
    return pl.pallas_call(
        prepare_kernel,
        out_shape=(
            jax.ShapeDtypeStruct((SENT, D), jnp.bfloat16),
            jax.ShapeDtypeStruct((1, RB), jnp.int32),
        ),
        name="prepare",
    )(embeds, member.reshape(1, RB))


def meet_kernel(total, rows, pairs, itself, lists, table, *refs):
    blocks, refs = refs[:total], refs[total:]
    if lists:
        where_ref, refs = refs[0], refs[1:]
        before, refs = refs[: len(lists) - 1], refs[len(lists) - 1 :]
    out_ref, held, across, down, row_best, column_best, sems = refs
    copies = []
    for k in range(total):
        copies.append(pltpu.make_async_copy(blocks[k], held.at[k], sems.at[k]))
        copies[k].start()
    row_best[...] = jnp.full_like(row_best, LOW)
    column_best[...] = jnp.full_like(column_best, LOW)
    if lists:
        out_ref[...] = jnp.full_like(out_ref, ABSENT)
    for k in range(total):
        copies[k].wait()
        clusters = held[k, RB:SENT, 0:RB].astype(jnp.float32)[0:8]
        across[k] = clusters
        if k < rows:
            down[k] = jnp.transpose(jnp.broadcast_to(clusters[0:1], (128, RB)))

    def meet(i, j, same):
        scores = lax.dot_general(
            held[i, 0:RB, :],
            held[j, 0:RB, :],
            (((1,), (1,)), ((), ())),
            preferred_element_type=jnp.float32,
        )
        keep = jnp.concatenate([down[i]] * (RB // 128), axis=1) == across[j, 0:1, :]
        if same:
            one = lax.broadcasted_iota(jnp.int32, (RB, RB), 0)
            keep = keep & (one != lax.broadcasted_iota(jnp.int32, (RB, RB), 1))
        scores = jnp.where(keep, scores, LOW)
        most = scores[:, 0:128]
        for q in range(1, RB // 128):
            most = jnp.maximum(most, scores[:, 128 * q : 128 * q + 128])
        row_best[i] = jnp.maximum(row_best[i], most)
        top = jnp.max(scores.reshape(RB // 8, 8, RB), axis=0)
        column_best[j] = jnp.maximum(column_best[j], top)

    if itself:
        meet(0, 0, True)

    def some(step, carry):
        for u in range(UNROLL):
            p = step * UNROLL + u
            meet(table[0, p], table[1, p], False)
        return carry

    lax.fori_loop(0, pairs // UNROLL, some, 0)
    for p in range(pairs // UNROLL * UNROLL, pairs):
        meet(table[0, p], table[1, p], False)

    def found_in(k):
        found = jnp.max(column_best[k], axis=0, keepdims=True)
        if k < rows:
            turned = jnp.transpose(row_best[k])
            found = jnp.maximum(found, jnp.max(turned, axis=0, keepdims=True))
        return found

    if not lists:
        for k in range(total):
            out_ref[k : k + 1, :] = found_in(k)
        return
    for number, name in enumerate(NAMES):
        found = jnp.full((1, RB), ABSENT, jnp.float32)
        if name in lists[0]:
            found = jnp.maximum(found, found_in(lists[0].index(name)))
        for ref, names in zip(before, lists[1:]):
            if name in names:
                at = names.index(name)
                found = jnp.maximum(found, ref[at : at + 1, :])
        out_ref[where_ref[number]] = found


def meet(held, meeting, lists=(), where=None, before=()):
    rows, names = members(meeting)
    pairs = [(i, j) for i, partners in meeting for j in partners]
    itself = (0, 0) in pairs
    pairs = [(names.index(i), names.index(j)) for i, j in pairs if i != j]
    total = len(names)
    shape = (128, 1, RB) if lists else (total, RB)
    in_specs = [pl.BlockSpec(memory_space=pltpu.SMEM)]
    in_specs += [pl.BlockSpec(memory_space=pl.ANY)] * total
    if lists:
        in_specs += [pl.BlockSpec(memory_space=pltpu.SMEM)]
        in_specs += [pl.BlockSpec(memory_space=pltpu.VMEM)] * len(before)
    return pl.pallas_call(
        functools.partial(meet_kernel, total, len(rows), len(pairs), itself, lists),
        out_shape=jax.ShapeDtypeStruct(shape, jnp.float32),
        in_specs=in_specs,
        scratch_shapes=[
            pltpu.VMEM((total, SENT, D), jnp.bfloat16),
            pltpu.VMEM((total, 8, RB), jnp.float32),
            pltpu.VMEM((len(rows), RB, 128), jnp.float32),
            pltpu.VMEM((len(rows), RB, 128), jnp.float32),
            pltpu.VMEM((total, 8, RB), jnp.float32),
            pltpu.SemaphoreType.DMA((total,)),
        ],
        compiler_params=pltpu.CompilerParams(vmem_limit_bytes=40 * 2**20),
        cost_estimate=pl.CostEstimate(
            flops=2 * RB * RB * D * len(pairs),
            bytes_accessed=total * SENT * D * 2,
            transcendentals=0,
        ),
        name=f"meet_{len(pairs)}",
    )(
        jnp.asarray(np.array(pairs, np.int32).T),
        *[held[k] for k in names],
        *(() if where is None else (where,)),
        *before,
    )


def finish_kernel(arrived_ref, target_ref, out_ref):
    best = jnp.max(arrived_ref[...], axis=0, keepdims=True)
    column = jnp.transpose(jnp.broadcast_to(best, (128, RB)))[:, 0:1]
    above = lax.broadcasted_iota(jnp.int32, (RB, RB), 0)
    picked = jnp.where(above == target_ref[...], column, LOW)
    out_ref[...] = jnp.max(picked, axis=0, keepdims=True)


def finish(arrived, target):
    return pl.pallas_call(
        finish_kernel, out_shape=jax.ShapeDtypeStruct((1, RB), jnp.float32), name="finish"
    )(arrived, target)


def homes():
    group, row = lax.axis_index("group"), lax.axis_index("row")
    x, y, z, core = group % 4, (group // 4) * 2 + (row // 2) % 2, row // 4, row % 2
    table = jnp.array(offsets(), jnp.int32)
    own = jnp.where(core == 0, table[0], table[1])
    other = jnp.where(core == 0, table[1], table[0])
    names = np.array(NAMES)
    steps = jnp.where((names < OTHER)[:, None], own[names % OTHER], other[names % OTHER])
    cores = jnp.where(names < OTHER, core, 1 - core)
    at = place((x + steps[:, 0]) % 4, (y + steps[:, 1]) % 4, (z + steps[:, 2]) % 4, cores)
    return at.astype(jnp.int32)


def on_device(embeds, member):
    block, target = prepare(embeds, member)
    held = {0: block}
    for i in range(1, SLOTS):
        held[i] = fetch(held[PARENT[i]], (UNIT[DIRS[0][i]], UNIT[DIRS[1][i]]))
    for name in NAMES:
        if name >= OTHER:
            held[name] = flip(held[name - OTHER])
    before = [meet(held, meeting) for meeting in MEETINGS[:-1]]
    lists = tuple(members(meeting)[1] for meeting in (MEETINGS[-1],) + MEETINGS[:-1])
    outgoing = meet(held, MEETINGS[-1], lists, homes(), before)
    arrived = lax.all_to_all(outgoing, AXES, split_axis=0, concat_axis=0, tiled=True)
    return finish(arrived.reshape(128, RB), target).reshape(-1)


def solution(mesh):
    in_specs = (P(AXES, None), P(AXES))
    return jax.shard_map(
        on_device, mesh=mesh, in_specs=in_specs, out_specs=P(AXES), check_vma=False
    )
```

```python
import functools

import jax
import jax.numpy as jnp
import numpy as np
from jax import lax
from jax.experimental import pallas as pl
from jax.experimental.pallas import tpu as pltpu
from jax.sharding import PartitionSpec as P

D = 768
RB = 512
GROUPS = 8
META = 16
SENT = RB + META
UNROLL = 4
ABSENT = -4.0
LOW = -1e30
AXES = ("group", "row")

UNIT = ((1, 0, 0), (0, 1, 0), (0, 0, 1), (3, 0, 0), (0, 3, 0), (0, 0, 3))
PARENT = (None,) + (0, 0, 0, 2, 1, 3, 6, 4, 4, 5, 5, 7)
DIRS = (
    (None,) + (5, 0, 2, 1, 3, 4, 0, 5, 1, 5, 2, 0),
    (None,) + (4, 3, 1, 2, 0, 5, 3, 4, 2, 4, 1, 3),
)
SLOTS = len(PARENT)
OTHER = 20
MEETINGS = (
    ((0, (0, 20)), (1, (0, 20, 21)), (2, (0, 1, 20, 21)), (3, (1, 2, 20, 21))),
    (
        (4, (0, 1, 2, 3, 21, 22)),
        (5, (2, 3, 4, 20, 21, 23, 24, 25)),
        (6, (0, 1, 4, 5, 20, 22, 23, 25, 26)),
    ),
    (
        (7, (0, 3, 4, 5, 21, 22, 23, 24, 26, 27)),
        (8, (3, 5, 6, 7, 20, 21, 24, 25, 27)),
        (9, (0, 1, 2, 5, 6, 8, 22, 26, 27)),
    ),
    ((10, (2, 9, 20, 21, 23)), (11, (2, 8, 9, 20, 26)), (12, (23, 27))),
)


def members(meeting):
    rows = tuple(k for k, partners in meeting)
    rest = sorted({k for row, partners in meeting for k in partners} - set(rows))
    return rows, rows + tuple(rest)


NAMES = tuple(sorted({k for meeting in MEETINGS for k in members(meeting)[1]}))


def offsets():
    table = []
    for core in range(2):
        held = [(0, 0, 0)]
        for i in range(1, SLOTS):
            step, base = UNIT[DIRS[core][i]], held[PARENT[i]]
            held.append(tuple((a + b) % 4 for a, b in zip(step, base)))
        table.append(held)
    return table


def place(x, y, z, core):
    group = (y // 2) * 4 + x
    row = (z * 2 + y % 2) * 2 + core
    return group * 16 + row


def fetch(block, steps):
    pairs = []
    for x in range(4):
        for y in range(4):
            for z in range(4):
                for core in range(2):
                    dx, dy, dz = steps[core]
                    source = place((x + dx) % 4, (y + dy) % 4, (z + dz) % 4, core)
                    pairs.append((source, place(x, y, z, core)))
    return lax.ppermute(block, AXES, sorted(pairs))


def flip(block):
    return lax.ppermute(block, AXES, [(i, i ^ 1) for i in range(128)])


def home(name, group, row):
    x, y, z = lax.rem(group, 4), lax.div(group, 4) * 2 + lax.rem(lax.div(row, 2), 2), lax.div(row, 4)
    core = lax.rem(row, 2)
    table = offsets()
    swap = 1 if name >= OTHER else 0
    at = []
    for axis, here in enumerate((x, y, z)):
        first = table[swap][name % OTHER][axis]
        second = table[1 - swap][name % OTHER][axis]
        at.append(lax.rem(here + jnp.where(core == 0, first, second), 4))
    core = 1 - core if swap else core
    group = lax.div(at[1], 2) * 4 + at[0]
    return group * 16 + (at[2] * 2 + lax.rem(at[1], 2)) * 2 + core


def prepare_kernel(embeds_ref, member_ref, block_ref, target_ref):
    member = member_ref[...].astype(jnp.float32)
    column = jnp.transpose(jnp.broadcast_to(member, (128, RB)))[:, 0:1]
    above = lax.broadcasted_iota(jnp.int32, (RB, RB), 0)
    across = lax.broadcasted_iota(jnp.int32, (RB, RB), 1)
    before = (column < member) | ((column == member) & (above < across))
    target = jnp.sum(before.astype(jnp.float32), axis=0, keepdims=True).astype(jnp.int32)
    target_ref[...] = target
    values = embeds_ref[...].astype(jnp.float32)
    total = jnp.sum(values * values, axis=1, keepdims=True)
    normed = (values * lax.rsqrt(total + 1e-06)).astype(jnp.bfloat16)
    placer = (above == target).astype(jnp.bfloat16)
    block_ref[0:RB, :] = jnp.dot(placer, normed, preferred_element_type=jnp.float32).astype(
        jnp.bfloat16
    )
    ordered = jnp.sum(jnp.where(above == target, member, 0.0), axis=1, keepdims=True)
    ordered = jnp.transpose(jnp.broadcast_to(ordered, (RB, 128)))[0:META]
    block_ref[RB:SENT, :] = jnp.zeros((META, D), jnp.bfloat16)
    block_ref[RB:SENT, 0:RB] = ordered.astype(jnp.bfloat16)


def prepare(embeds, member):
    return pl.pallas_call(
        prepare_kernel,
        out_shape=(
            jax.ShapeDtypeStruct((SENT, D), jnp.bfloat16),
            jax.ShapeDtypeStruct((1, RB), jnp.int32),
        ),
        name="prepare",
    )(embeds, member.reshape(1, RB))


def meet_kernel(total, rows, pairs, itself, lists, table, waits, *refs):
    blocks, refs = refs[:total], refs[total:]
    if lists:
        place_ref, refs = refs[0], refs[1:]
        before, refs = refs[: len(lists) - 1], refs[len(lists) - 1 :]
    out_ref, held, across, down, row_best, column_best, sems = refs
    for k in range(total):
        pltpu.make_async_copy(blocks[k], held.at[k], sems.at[k]).start()
    row_best[...] = jnp.full_like(row_best, LOW)
    column_best[...] = jnp.full_like(column_best, LOW)
    if lists:
        out_ref[...] = jnp.full_like(out_ref, ABSENT)
    def arrive(k):
        pltpu.make_async_copy(blocks[0], held.at[k], sems.at[k]).wait()
        across[k] = held[k, RB:SENT, 0:RB].astype(jnp.float32)[0:8]

    for k in range(rows):
        arrive(k)
        down[k] = jnp.transpose(jnp.broadcast_to(across[k, 0:1], (128, RB)))

    def meet(i, j, same):
        scores = lax.dot_general(
            held[i, 0:RB, :],
            held[j, 0:RB, :],
            (((1,), (1,)), ((), ())),
            preferred_element_type=jnp.float32,
        )
        keep = jnp.concatenate([down[i]] * (RB // 128), axis=1) == across[j, 0:1, :]
        if same:
            one = lax.broadcasted_iota(jnp.int32, (RB, RB), 0)
            keep = keep & (one != lax.broadcasted_iota(jnp.int32, (RB, RB), 1))
        scores = jnp.where(keep, scores, LOW)
        most = scores[:, 0:128]
        for q in range(1, RB // 128):
            most = jnp.maximum(most, scores[:, 128 * q : 128 * q + 128])
        row_best[i] = jnp.maximum(row_best[i], most)
        top = jnp.max(scores.reshape(RB // 8, 8, RB), axis=0)
        column_best[j] = jnp.maximum(column_best[j], top)

    if itself:
        meet(0, 0, True)

    def await_step(step, length):
        for u in range(length):
            block = waits[step * UNROLL + u]
            pl.when(block >= 0)(functools.partial(arrive, block))

    def some(step, carry):
        await_step(step, UNROLL)
        for u in range(UNROLL):
            p = step * UNROLL + u
            meet(table[0, p], table[1, p], False)
        return carry

    steps = pairs // UNROLL
    lax.fori_loop(0, steps, some, 0)
    await_step(steps, pairs - steps * UNROLL)
    for p in range(steps * UNROLL, pairs):
        meet(table[0, p], table[1, p], False)

    def found_in(k):
        found = jnp.max(column_best[k], axis=0, keepdims=True)
        if k < rows:
            turned = jnp.transpose(row_best[k])
            found = jnp.maximum(found, jnp.max(turned, axis=0, keepdims=True))
        return found

    if not lists:
        for k in range(total):
            out_ref[k : k + 1, :] = found_in(k)
        return
    for number, name in enumerate(NAMES):
        found = jnp.full((1, RB), ABSENT, jnp.float32)
        if name in lists[0]:
            found = jnp.maximum(found, found_in(lists[0].index(name)))
        for ref, names in zip(before, lists[1:]):
            if name in names:
                at = names.index(name)
                found = jnp.maximum(found, ref[at : at + 1, :])
        out_ref[home(name, place_ref[0], place_ref[1])] = found


def meet(held, meeting, lists=(), before=()):
    rows, names = members(meeting)
    pairs = [(i, j) for i, partners in meeting for j in partners]
    itself = (0, 0) in pairs
    pairs = sorted(
        ((names.index(i), names.index(j)) for i, j in pairs if i != j), key=lambda p: p[::-1]
    )
    seen, waits = set(range(len(rows))), []
    for i, j in pairs:
        waits.append(-1 if j in seen else j)
        seen.add(j)
    total = len(names)
    shape = (128, 1, RB) if lists else (total, RB)
    in_specs = [pl.BlockSpec(memory_space=pltpu.SMEM)] * 2
    in_specs += [pl.BlockSpec(memory_space=pl.ANY)] * total
    if lists:
        in_specs += [pl.BlockSpec(memory_space=pltpu.SMEM)]
        in_specs += [pl.BlockSpec(memory_space=pltpu.VMEM)] * len(before)
    return pl.pallas_call(
        functools.partial(meet_kernel, total, len(rows), len(pairs), itself, lists),
        out_shape=jax.ShapeDtypeStruct(shape, jnp.float32),
        in_specs=in_specs,
        scratch_shapes=[
            pltpu.VMEM((total, SENT, D), jnp.bfloat16),
            pltpu.VMEM((total, 8, RB), jnp.float32),
            pltpu.VMEM((len(rows), RB, 128), jnp.float32),
            pltpu.VMEM((len(rows), RB, 128), jnp.float32),
            pltpu.VMEM((total, 8, RB), jnp.float32),
            pltpu.SemaphoreType.DMA((total,)),
        ],
        compiler_params=pltpu.CompilerParams(vmem_limit_bytes=58 * 2**20),
        cost_estimate=pl.CostEstimate(
            flops=2 * RB * RB * D * len(pairs),
            bytes_accessed=total * SENT * D * 2,
            transcendentals=0,
        ),
        name=f"meet_{len(pairs)}",
    )(
        jnp.asarray(np.array(pairs, np.int32).T),
        jnp.asarray(np.array(waits, np.int32)),
        *[held[k] for k in names],
        *((jnp.stack([lax.axis_index(axis) for axis in AXES]),) if lists else ()),
        *before,
    )


def finish_kernel(arrived_ref, target_ref, out_ref):
    best = jnp.max(arrived_ref[...], axis=0)
    column = jnp.transpose(jnp.broadcast_to(best, (128, RB)))[:, 0:1]
    above = lax.broadcasted_iota(jnp.int32, (RB, RB), 0)
    picked = jnp.where(above == target_ref[...], column, LOW)
    out_ref[...] = jnp.max(picked, axis=0, keepdims=True)


def finish(arrived, target):
    return pl.pallas_call(
        finish_kernel, out_shape=jax.ShapeDtypeStruct((1, RB), jnp.float32), name="finish"
    )(arrived, target)


def on_device(embeds, member):
    block, target = prepare(embeds, member)
    held = {0: block}
    before = []

    def go(first):
        for i in range(first, first + 3):
            held[i] = fetch(held[PARENT[i]], (UNIT[DIRS[0][i]], UNIT[DIRS[1][i]]))

    def share(slots):
        for i in slots:
            if i + OTHER in NAMES:
                held[i + OTHER] = flip(held[i])

    def after(slots):
        kept = lax.optimization_barrier((before[-1], *[held[i] for i in slots]))
        before[-1] = kept[0]
        held.update(zip(slots, kept[1:]))

    go(1)
    share((0, 1))
    go(4)
    before.append(meet(held, MEETINGS[0]))
    after((2, 3, 4, 5, 6))
    go(7)
    share((2, 3, 4, 5, 6))
    before.append(meet(held, MEETINGS[1]))
    after((7, 8, 9))
    go(10)
    share((7, 8, 9))
    before.append(meet(held, MEETINGS[2]))
    lists = tuple(members(meeting)[1] for meeting in (MEETINGS[-1],) + MEETINGS[:-1])
    outgoing = meet(held, MEETINGS[-1], lists, before)
    arrived = lax.all_to_all(outgoing, AXES, split_axis=0, concat_axis=0, tiled=True)
    return finish(arrived, target).reshape(-1)


def solution(mesh):
    in_specs = (P(AXES, None), P(AXES))
    return jax.shard_map(
        on_device, mesh=mesh, in_specs=in_specs, out_specs=P(AXES), check_vma=False
    )
```

```python
import functools

import jax
import jax.numpy as jnp
import numpy as np
from jax import lax
from jax.experimental import pallas as pl
from jax.experimental.pallas import tpu as pltpu
from jax.sharding import PartitionSpec as P

D = 768
RB = 512
GROUPS = 8
META = 16
SENT = RB + META
UNROLL = 4
HALF = 256
BAND = 384
ABSENT = -4.0
LOW = -1e30
AXES = ("group", "row")

UNIT = ((1, 0, 0), (0, 1, 0), (0, 0, 1), (3, 0, 0), (0, 3, 0), (0, 0, 3))
PARENT = (None,) + (0, 0, 0, 2, 1, 3, 6, 4, 4, 5, 5, 7)
DIRS = (
    (None,) + (5, 0, 2, 1, 3, 4, 0, 5, 1, 5, 2, 0),
    (None,) + (4, 3, 1, 2, 0, 5, 3, 4, 2, 4, 1, 3),
)
SLOTS = len(PARENT)
OTHER = 20
MEETINGS = (
    ((0, (0, 20)), (1, (0, 20, 21)), (2, (0, 1, 20, 21)), (3, (1, 2, 20, 21))),
    (
        (4, (0, 1, 2, 3, 21, 22)),
        (5, (2, 3, 4, 20, 21, 23, 24, 25)),
        (6, (0, 1, 4, 5, 20, 22, 23, 25, 26)),
    ),
    (
        (7, (0, 3, 4, 5, 21, 22, 23, 24, 26, 27)),
        (8, (3, 5, 6, 7, 20, 21, 24, 25, 27)),
        (9, (0, 1, 2, 5, 6, 8, 22, 26, 27)),
    ),
    ((10, (2, 9, 20, 21, 23)), (11, (2, 8, 9, 20, 26)), (12, (23, 27))),
)


def members(meeting):
    rows = tuple(k for k, partners in meeting)
    rest = sorted({k for row, partners in meeting for k in partners} - set(rows))
    return rows, rows + tuple(rest)


NAMES = tuple(sorted({k for meeting in MEETINGS for k in members(meeting)[1]}))


def offsets():
    table = []
    for core in range(2):
        held = [(0, 0, 0)]
        for i in range(1, SLOTS):
            step, base = UNIT[DIRS[core][i]], held[PARENT[i]]
            held.append(tuple((a + b) % 4 for a, b in zip(step, base)))
        table.append(held)
    return table


def place(x, y, z, core):
    group = (y // 2) * 4 + x
    row = (z * 2 + y % 2) * 2 + core
    return group * 16 + row


def fetch(block, steps):
    pairs = []
    for x in range(4):
        for y in range(4):
            for z in range(4):
                for core in range(2):
                    dx, dy, dz = steps[core]
                    source = place((x + dx) % 4, (y + dy) % 4, (z + dz) % 4, core)
                    pairs.append((source, place(x, y, z, core)))
    return lax.ppermute(block, AXES, sorted(pairs))


def flip(block):
    return lax.ppermute(block, AXES, [(i, i ^ 1) for i in range(128)])


def home(name, group, row):
    x, y, z = lax.rem(group, 4), lax.div(group, 4) * 2 + lax.rem(lax.div(row, 2), 2), lax.div(row, 4)
    core = lax.rem(row, 2)
    table = offsets()
    swap = 1 if name >= OTHER else 0
    at = []
    for axis, here in enumerate((x, y, z)):
        first = table[swap][name % OTHER][axis]
        second = table[1 - swap][name % OTHER][axis]
        at.append(lax.rem(here + jnp.where(core == 0, first, second), 4))
    core = 1 - core if swap else core
    group = lax.div(at[1], 2) * 4 + at[0]
    return group * 16 + (at[2] * 2 + lax.rem(at[1], 2)) * 2 + core


def prepare_kernel(embeds_ref, member_ref, block_ref, target_ref):
    member = member_ref[...].astype(jnp.float32)
    column = jnp.transpose(jnp.broadcast_to(member, (128, RB)))[:, 0:1]
    above = lax.broadcasted_iota(jnp.int32, (RB, RB), 0)
    across = lax.broadcasted_iota(jnp.int32, (RB, RB), 1)
    before = (column < member) | ((column == member) & (above < across))
    target = jnp.sum(before.astype(jnp.float32), axis=0, keepdims=True).astype(jnp.int32)
    target_ref[...] = target
    values = embeds_ref[...].astype(jnp.float32)
    total = jnp.sum(values * values, axis=1, keepdims=True)
    normed = (values * lax.rsqrt(total + 1e-06)).astype(jnp.bfloat16)
    placer = (above == target).astype(jnp.bfloat16)
    block_ref[0:RB, :] = jnp.dot(placer, normed, preferred_element_type=jnp.float32).astype(
        jnp.bfloat16
    )
    ordered = jnp.sum(jnp.where(above == target, member, 0.0), axis=1, keepdims=True)
    ordered = jnp.transpose(jnp.broadcast_to(ordered, (RB, 128)))[0:META]
    block_ref[RB:SENT, :] = jnp.zeros((META, D), jnp.bfloat16)
    block_ref[RB:SENT, 0:RB] = ordered.astype(jnp.bfloat16)


def prepare(embeds, member):
    return pl.pallas_call(
        prepare_kernel,
        out_shape=(
            jax.ShapeDtypeStruct((SENT, D), jnp.bfloat16),
            jax.ShapeDtypeStruct((1, RB), jnp.int32),
        ),
        name="prepare",
    )(embeds, member.reshape(1, RB))


def meet_kernel(total, rows, pairs, itself, lists, table, waits, *refs):
    blocks, refs = refs[:total], refs[total:]
    if lists:
        place_ref, refs = refs[0], refs[1:]
        before, refs = refs[: len(lists) - 1], refs[len(lists) - 1 :]
    out_ref, held, across, down, row_best, column_best, sems = refs
    for k in range(total):
        pltpu.make_async_copy(blocks[k], held.at[k], sems.at[k]).start()
    row_best[...] = jnp.full_like(row_best, LOW)
    column_best[...] = jnp.full_like(column_best, LOW)
    if lists:
        out_ref[...] = jnp.full_like(out_ref, ABSENT)
    def arrive(k):
        pltpu.make_async_copy(blocks[0], held.at[k], sems.at[k]).wait()
        across[k] = held[k, RB:SENT, 0:RB].astype(jnp.float32)[0:8]

    for k in range(rows):
        arrive(k)
        down[k] = jnp.transpose(jnp.broadcast_to(across[k, 0:1], (128, RB)))

    def meet(i, j, at, length, column, width, same):
        scores = lax.dot_general(
            held[i, at : at + length, :],
            held[j, column : column + width, :],
            (((1,), (1,)), ((), ())),
            preferred_element_type=jnp.float32,
        )
        here = jnp.concatenate([down[i, at : at + length, :]] * (width // 128), axis=1)
        keep = here == across[j, 0:1, column : column + width]
        if same:
            one = lax.broadcasted_iota(jnp.int32, (length, width), 0)
            keep = keep & (one != lax.broadcasted_iota(jnp.int32, (length, width), 1))
        scores = jnp.where(keep, scores, LOW)
        most = scores[:, 0:128]
        for q in range(1, width // 128):
            most = jnp.maximum(most, scores[:, 128 * q : 128 * q + 128])
        row_best[i, at : at + length, :] = jnp.maximum(row_best[i, at : at + length, :], most)
        top = jnp.max(scores.reshape(length // 8, 8, width), axis=0)
        span = slice(column, column + width)
        column_best[j, :, span] = jnp.maximum(column_best[j, :, span], top)

    def near(i, j):
        meet(i, j, 0, BAND, 0, HALF, False)
        meet(i, j, RB - BAND, BAND, HALF, HALF, False)

    def far(i, j):
        late = across[j, 0:1, HALF - 128 : HALF] >= down[i, BAND : BAND + 1, :]
        early = across[j, 0:1, HALF : HALF + 128] <= down[i, RB - BAND - 1 : RB - BAND, :]
        return jnp.where(late | early, 1.0, 0.0)

    def visit(first, length):
        pairs_here = [(table[0, first + u], table[1, first + u]) for u in range(length)]
        flags = functools.reduce(jnp.maximum, [far(i, j) for i, j in pairs_here])
        flag = jnp.max(flags)
        for i, j in pairs_here:
            near(i, j)

        @pl.when(flag > 0.0)
        def _():
            def rest(p, carry):
                i, j = table[0, p], table[1, p]
                meet(i, j, BAND, RB - BAND, 0, HALF, False)
                meet(i, j, 0, RB - BAND, HALF, HALF, False)
                return carry

            lax.fori_loop(first, first + length, rest, 0)

    if itself:
        meet(0, 0, 0, RB, 0, RB, True)

    def await_step(step, length):
        for u in range(length):
            block = waits[step * UNROLL + u]
            pl.when(block >= 0)(functools.partial(arrive, block))

    def some(step, carry):
        await_step(step, UNROLL)
        visit(step * UNROLL, UNROLL)
        return carry

    steps = pairs // UNROLL
    lax.fori_loop(0, steps, some, 0)
    if pairs > steps * UNROLL:
        await_step(steps, pairs - steps * UNROLL)
        visit(steps * UNROLL, pairs - steps * UNROLL)

    def found_in(k):
        found = jnp.max(column_best[k], axis=0, keepdims=True)
        if k < rows:
            turned = jnp.transpose(row_best[k])
            found = jnp.maximum(found, jnp.max(turned, axis=0, keepdims=True))
        return found

    if not lists:
        for k in range(total):
            out_ref[k : k + 1, :] = found_in(k)
        return
    for number, name in enumerate(NAMES):
        found = jnp.full((1, RB), ABSENT, jnp.float32)
        if name in lists[0]:
            found = jnp.maximum(found, found_in(lists[0].index(name)))
        for ref, names in zip(before, lists[1:]):
            if name in names:
                at = names.index(name)
                found = jnp.maximum(found, ref[at : at + 1, :])
        out_ref[home(name, place_ref[0], place_ref[1])] = found


def meet(held, meeting, lists=(), before=()):
    rows, names = members(meeting)
    pairs = [(i, j) for i, partners in meeting for j in partners]
    itself = (0, 0) in pairs
    pairs = sorted(
        ((names.index(i), names.index(j)) for i, j in pairs if i != j), key=lambda p: p[::-1]
    )
    seen, waits = set(range(len(rows))), []
    for i, j in pairs:
        waits.append(-1 if j in seen else j)
        seen.add(j)
    total = len(names)
    shape = (128, 1, RB) if lists else (total, RB)
    in_specs = [pl.BlockSpec(memory_space=pltpu.SMEM)] * 2
    in_specs += [pl.BlockSpec(memory_space=pltpu.HBM)] * total
    if lists:
        in_specs += [pl.BlockSpec(memory_space=pltpu.SMEM)]
        in_specs += [pl.BlockSpec(memory_space=pltpu.VMEM)] * len(before)
    return pl.pallas_call(
        functools.partial(meet_kernel, total, len(rows), len(pairs), itself, lists),
        out_shape=jax.ShapeDtypeStruct(shape, jnp.float32),
        in_specs=in_specs,
        scratch_shapes=[
            pltpu.VMEM((total, SENT, D), jnp.bfloat16),
            pltpu.VMEM((total, 8, RB), jnp.float32),
            pltpu.VMEM((len(rows), RB, 128), jnp.float32),
            pltpu.VMEM((len(rows), RB, 128), jnp.float32),
            pltpu.VMEM((total, 8, RB), jnp.float32),
            pltpu.SemaphoreType.DMA((total,)),
        ],
        compiler_params=pltpu.CompilerParams(vmem_limit_bytes=58 * 2**20),
        cost_estimate=pl.CostEstimate(
            flops=2 * RB * RB * D * len(pairs),
            bytes_accessed=total * SENT * D * 2,
            transcendentals=0,
        ),
        name=f"meet_{len(pairs)}",
    )(
        jnp.asarray(np.array(pairs, np.int32).T),
        jnp.asarray(np.array(waits, np.int32)),
        *[held[k] for k in names],
        *((jnp.stack([lax.axis_index(axis) for axis in AXES]),) if lists else ()),
        *before,
    )


def finish_kernel(arrived_ref, target_ref, out_ref):
    best = jnp.max(arrived_ref[...], axis=0)
    column = jnp.transpose(jnp.broadcast_to(best, (128, RB)))[:, 0:1]
    above = lax.broadcasted_iota(jnp.int32, (RB, RB), 0)
    picked = jnp.where(above == target_ref[...], column, LOW)
    out_ref[...] = jnp.max(picked, axis=0, keepdims=True)


def finish(arrived, target):
    return pl.pallas_call(
        finish_kernel, out_shape=jax.ShapeDtypeStruct((1, RB), jnp.float32), name="finish"
    )(arrived, target)


def on_device(embeds, member):
    block, target = prepare(embeds, member)
    held = {0: block}
    before = []

    def go(first):
        for i in range(first, first + 3):
            held[i] = fetch(held[PARENT[i]], (UNIT[DIRS[0][i]], UNIT[DIRS[1][i]]))

    def share(slots):
        for i in slots:
            if i + OTHER in NAMES:
                held[i + OTHER] = flip(held[i])

    def after(slots):
        kept = lax.optimization_barrier((before[-1], *[held[i] for i in slots]))
        before[-1] = kept[0]
        held.update(zip(slots, kept[1:]))

    go(1)
    share((0, 1))
    go(4)
    before.append(meet(held, MEETINGS[0]))
    after((2, 3, 4, 5, 6))
    go(7)
    share((2, 3, 4, 5, 6))
    before.append(meet(held, MEETINGS[1]))
    after((7, 8, 9))
    go(10)
    share((7, 8, 9))
    before.append(meet(held, MEETINGS[2]))
    lists = tuple(members(meeting)[1] for meeting in (MEETINGS[-1],) + MEETINGS[:-1])
    outgoing = meet(held, MEETINGS[-1], lists, before)
    arrived = lax.all_to_all(outgoing, AXES, split_axis=0, concat_axis=0, tiled=True)
    return finish(arrived, target).reshape(-1)


def solution(mesh):
    in_specs = (P(AXES, None), P(AXES))
    return jax.shard_map(
        on_device, mesh=mesh, in_specs=in_specs, out_specs=P(AXES), check_vma=False
    )
```

```python
import functools

import jax
import jax.numpy as jnp
import numpy as np
from jax import lax
from jax.experimental import pallas as pl
from jax.experimental.pallas import tpu as pltpu
from jax.sharding import PartitionSpec as P

D = 768
RB = 512
GROUPS = 8
META = 16
SENT = RB + META
UNROLL = 4
HALF = 256
BAND = 384
ABSENT = -4.0
LOW = -1e30
AXES = ("group", "row")

UNIT = ((1, 0, 0), (0, 1, 0), (0, 0, 1), (3, 0, 0), (0, 3, 0), (0, 0, 3))
PARENT = (None,) + (0, 0, 0, 2, 1, 3, 6, 4, 4, 5, 5, 7)
DIRS = (
    (None,) + (5, 0, 2, 1, 3, 4, 0, 5, 1, 5, 2, 0),
    (None,) + (4, 3, 1, 2, 0, 5, 3, 4, 2, 4, 1, 3),
)
SLOTS = len(PARENT)
OTHER = 20
MEETINGS = (
    ((0, (0, 20)), (1, (0, 20, 21)), (2, (0, 1, 20, 21)), (3, (1, 2, 20, 21))),
    (
        (4, (0, 1, 2, 3, 21, 22)),
        (5, (2, 3, 4, 20, 21, 23, 24, 25)),
        (6, (0, 1, 4, 5, 20, 22, 23, 25, 26)),
    ),
    (
        (7, (0, 3, 4, 5, 21, 22, 23, 24, 26, 27)),
        (8, (3, 5, 6, 7, 20, 21, 24, 25, 27)),
        (9, (0, 1, 2, 5, 6, 8, 22, 26, 27)),
    ),
    ((10, (2, 9, 20, 21, 23)), (11, (2, 8, 9, 20, 26)), (12, (23, 27))),
)


def members(meeting):
    rows = tuple(k for k, partners in meeting)
    rest = sorted({k for row, partners in meeting for k in partners} - set(rows))
    return rows, rows + tuple(rest)


NAMES = tuple(sorted({k for meeting in MEETINGS for k in members(meeting)[1]}))


def offsets():
    table = []
    for core in range(2):
        held = [(0, 0, 0)]
        for i in range(1, SLOTS):
            step, base = UNIT[DIRS[core][i]], held[PARENT[i]]
            held.append(tuple((a + b) % 4 for a, b in zip(step, base)))
        table.append(held)
    return table


def place(x, y, z, core):
    group = (y // 2) * 4 + x
    row = (z * 2 + y % 2) * 2 + core
    return group * 16 + row


def fetch(block, steps):
    pairs = []
    for x in range(4):
        for y in range(4):
            for z in range(4):
                for core in range(2):
                    dx, dy, dz = steps[core]
                    source = place((x + dx) % 4, (y + dy) % 4, (z + dz) % 4, core)
                    pairs.append((source, place(x, y, z, core)))
    return lax.ppermute(block, AXES, sorted(pairs))


def flip(block):
    return lax.ppermute(block, AXES, [(i, i ^ 1) for i in range(128)])


def home(name, group, row):
    x, y, z = lax.rem(group, 4), lax.div(group, 4) * 2 + lax.rem(lax.div(row, 2), 2), lax.div(row, 4)
    core = lax.rem(row, 2)
    table = offsets()
    swap = 1 if name >= OTHER else 0
    at = []
    for axis, here in enumerate((x, y, z)):
        first = table[swap][name % OTHER][axis]
        second = table[1 - swap][name % OTHER][axis]
        at.append(lax.rem(here + jnp.where(core == 0, first, second), 4))
    core = 1 - core if swap else core
    group = lax.div(at[1], 2) * 4 + at[0]
    return group * 16 + (at[2] * 2 + lax.rem(at[1], 2)) * 2 + core


def prepare_kernel(embeds_ref, member_ref, block_ref, target_ref):
    member = member_ref[...].astype(jnp.float32)
    column = jnp.transpose(jnp.broadcast_to(member, (128, RB)))[:, 0:1]
    above = lax.broadcasted_iota(jnp.int32, (RB, RB), 0)
    across = lax.broadcasted_iota(jnp.int32, (RB, RB), 1)
    before = (column < member) | ((column == member) & (above < across))
    target = jnp.sum(before.astype(jnp.float32), axis=0, keepdims=True).astype(jnp.int32)
    target_ref[...] = target
    values = embeds_ref[...].astype(jnp.float32)
    total = jnp.sum(values * values, axis=1, keepdims=True)
    normed = (values * lax.rsqrt(total + 1e-06)).astype(jnp.bfloat16)
    placer = (above == target).astype(jnp.bfloat16)
    block_ref[0:RB, :] = jnp.dot(placer, normed, preferred_element_type=jnp.float32).astype(
        jnp.bfloat16
    )
    ordered = jnp.sum(jnp.where(above == target, member, 0.0), axis=1, keepdims=True)
    ordered = jnp.transpose(jnp.broadcast_to(ordered, (RB, 128)))[0:META]
    block_ref[RB:SENT, :] = jnp.zeros((META, D), jnp.bfloat16)
    block_ref[RB:SENT, 0:RB] = ordered.astype(jnp.bfloat16)


def prepare(embeds, member):
    return pl.pallas_call(
        prepare_kernel,
        out_shape=(
            jax.ShapeDtypeStruct((SENT, D), jnp.bfloat16),
            jax.ShapeDtypeStruct((1, RB), jnp.int32),
        ),
        name="prepare",
    )(embeds, member.reshape(1, RB))


def meet_kernel(total, rows, pairs, itself, lists, fetched, *refs):
    blocks, refs = refs[:total], refs[total:]
    if lists:
        before, refs = refs[: len(lists) - 1], refs[len(lists) - 1 :]
    out_ref, held, across, down, row_best, column_best, table, waits, sems = refs
    for k in range(total):
        pltpu.make_async_copy(blocks[k], held.at[k], sems.at[k]).start()
    for p, (i, j) in enumerate(pairs):
        table[0, p] = i
        table[1, p] = j
        waits[p] = fetched[p]
    pairs = len(pairs)
    row_best[...] = jnp.full_like(row_best, LOW)
    column_best[...] = jnp.full_like(column_best, LOW)
    if lists:
        out_ref[...] = jnp.full_like(out_ref, ABSENT)

    def arrive(k):
        pltpu.make_async_copy(blocks[0], held.at[k], sems.at[k]).wait()
        across[k] = held[k, RB:SENT, 0:RB].astype(jnp.float32)[0:8]

    for k in range(rows):
        arrive(k)
        down[k] = jnp.transpose(jnp.broadcast_to(across[k, 0:1], (128, RB)))

    def meet(i, j, at, length, column, width, same):
        scores = lax.dot_general(
            held[i, at : at + length, :],
            held[j, column : column + width, :],
            (((1,), (1,)), ((), ())),
            preferred_element_type=jnp.float32,
        )
        here = jnp.concatenate([down[i, at : at + length, :]] * (width // 128), axis=1)
        keep = here == across[j, 0:1, column : column + width]
        if same:
            one = lax.broadcasted_iota(jnp.int32, (length, width), 0)
            keep = keep & (one != lax.broadcasted_iota(jnp.int32, (length, width), 1))
        scores = jnp.where(keep, scores, LOW)
        most = scores[:, 0:128]
        for q in range(1, width // 128):
            most = jnp.maximum(most, scores[:, 128 * q : 128 * q + 128])
        row_best[i, at : at + length, :] = jnp.maximum(row_best[i, at : at + length, :], most)
        top = jnp.max(scores.reshape(length // 8, 8, width), axis=0)
        span = slice(column, column + width)
        column_best[j, :, span] = jnp.maximum(column_best[j, :, span], top)

    def near(i, j):
        meet(i, j, 0, BAND, 0, HALF, False)
        meet(i, j, RB - BAND, BAND, HALF, HALF, False)

    def far(i, j):
        late = across[j, 0:1, HALF - 128 : HALF] >= down[i, BAND : BAND + 1, :]
        early = across[j, 0:1, HALF : HALF + 128] <= down[i, RB - BAND - 1 : RB - BAND, :]
        return jnp.where(late | early, 1.0, 0.0)

    def visit(first, length):
        pairs_here = [(table[0, first + u], table[1, first + u]) for u in range(length)]
        flags = functools.reduce(jnp.maximum, [far(i, j) for i, j in pairs_here])
        flag = jnp.max(flags)
        for i, j in pairs_here:
            near(i, j)

        @pl.when(flag > 0.0)
        def _():
            def rest(p, carry):
                i, j = table[0, p], table[1, p]
                meet(i, j, BAND, RB - BAND, 0, HALF, False)
                meet(i, j, 0, RB - BAND, HALF, HALF, False)
                return carry

            lax.fori_loop(first, first + length, rest, 0)

    if itself:
        meet(0, 0, 0, RB, 0, RB, True)

    def await_step(step, length):
        for u in range(length):
            block = waits[step * UNROLL + u]
            pl.when(block >= 0)(functools.partial(arrive, block))

    def some(step, carry):
        await_step(step, UNROLL)
        visit(step * UNROLL, UNROLL)
        return carry

    steps = pairs // UNROLL
    lax.fori_loop(0, steps, some, 0)
    if pairs > steps * UNROLL:
        await_step(steps, pairs - steps * UNROLL)
        visit(steps * UNROLL, pairs - steps * UNROLL)

    def found_in(k):
        found = jnp.max(column_best[k], axis=0, keepdims=True)
        if k < rows:
            turned = jnp.transpose(row_best[k])
            found = jnp.maximum(found, jnp.max(turned, axis=0, keepdims=True))
        return found

    if not lists:
        for k in range(total):
            out_ref[k : k + 1, :] = found_in(k)
        return
    here = [lax.axis_index(axis) for axis in AXES]
    for name in NAMES:
        found = jnp.full((1, RB), ABSENT, jnp.float32)
        if name in lists[0]:
            found = jnp.maximum(found, found_in(lists[0].index(name)))
        for ref, names in zip(before, lists[1:]):
            if name in names:
                at = names.index(name)
                found = jnp.maximum(found, ref[at : at + 1, :])
        out_ref[home(name, *here)] = found


def meet(held, meeting, lists=(), before=()):
    rows, names = members(meeting)
    pairs = [(i, j) for i, partners in meeting for j in partners]
    itself = (0, 0) in pairs
    pairs = sorted(
        ((names.index(i), names.index(j)) for i, j in pairs if i != j), key=lambda p: p[::-1]
    )
    seen, waits = set(range(len(rows))), []
    for i, j in pairs:
        waits.append(-1 if j in seen else j)
        seen.add(j)
    total = len(names)
    shape = (128, 1, RB) if lists else (total, RB)
    in_specs = [pl.BlockSpec(memory_space=pltpu.HBM)] * total
    if lists:
        in_specs += [pl.BlockSpec(memory_space=pltpu.VMEM)] * len(before)
    return pl.pallas_call(
        functools.partial(meet_kernel, total, len(rows), pairs, itself, lists, waits),
        out_shape=jax.ShapeDtypeStruct(shape, jnp.float32),
        in_specs=in_specs,
        scratch_shapes=[
            pltpu.VMEM((total, SENT, D), jnp.bfloat16),
            pltpu.VMEM((total, 8, RB), jnp.float32),
            pltpu.VMEM((len(rows), RB, 128), jnp.float32),
            pltpu.VMEM((len(rows), RB, 128), jnp.float32),
            pltpu.VMEM((total, 8, RB), jnp.float32),
            pltpu.SMEM((2, len(pairs)), jnp.int32),
            pltpu.SMEM((len(pairs),), jnp.int32),
            pltpu.SemaphoreType.DMA((total,)),
        ],
        compiler_params=pltpu.CompilerParams(vmem_limit_bytes=66_400_000),
        cost_estimate=pl.CostEstimate(
            flops=2 * RB * RB * D * len(pairs),
            bytes_accessed=total * SENT * D * 2,
            transcendentals=0,
        ),
        name=f"meet_{len(pairs)}",
    )(
        *[held[k] for k in names],
        *before,
    )


def finish_kernel(arrived_ref, target_ref, out_ref):
    best = jnp.max(arrived_ref[...], axis=0)
    column = jnp.transpose(jnp.broadcast_to(best, (128, RB)))[:, 0:1]
    above = lax.broadcasted_iota(jnp.int32, (RB, RB), 0)
    picked = jnp.where(above == target_ref[...], column, LOW)
    out_ref[...] = jnp.max(picked, axis=0, keepdims=True)


def finish(arrived, target):
    return pl.pallas_call(
        finish_kernel, out_shape=jax.ShapeDtypeStruct((1, RB), jnp.float32), name="finish"
    )(arrived, target)


def on_device(embeds, member):
    block, target = prepare(embeds, member)
    held = {0: block}
    before = []

    def go(first):
        for i in range(first, first + 3):
            held[i] = fetch(held[PARENT[i]], (UNIT[DIRS[0][i]], UNIT[DIRS[1][i]]))

    def share(slots):
        for i in slots:
            if i + OTHER in NAMES:
                held[i + OTHER] = flip(held[i])

    def after(slots):
        kept = lax.optimization_barrier((before[-1], *[held[i] for i in slots]))
        before[-1] = kept[0]
        held.update(zip(slots, kept[1:]))

    go(1)
    share((0, 1))
    go(4)
    before.append(meet(held, MEETINGS[0]))
    after((2, 3, 4, 5, 6))
    go(7)
    share((2, 3, 4, 5, 6))
    before.append(meet(held, MEETINGS[1]))
    after((7, 8, 9))
    go(10)
    share((7, 8, 9))
    before.append(meet(held, MEETINGS[2]))
    lists = tuple(members(meeting)[1] for meeting in (MEETINGS[-1],) + MEETINGS[:-1])
    outgoing = meet(held, MEETINGS[-1], lists, before)
    arrived = lax.all_to_all(outgoing, AXES, split_axis=0, concat_axis=0, tiled=True)
    return finish(arrived, target).reshape(-1)


def solution(mesh):
    in_specs = (P(AXES, None), P(AXES))
    return jax.shard_map(
        on_device, mesh=mesh, in_specs=in_specs, out_specs=P(AXES), check_vma=False
    )
```

```python
import functools

import jax
import jax.numpy as jnp
import numpy as np
from jax import lax
from jax.experimental import pallas as pl
from jax.experimental.pallas import tpu as pltpu
from jax.sharding import PartitionSpec as P

D = 768
RB = 512
GROUPS = 8
META = 16
SENT = RB + META
UNROLL = 4
HALF = 256
BAND = 384
ABSENT = -4.0
LOW = -1e30
AXES = ("group", "row")

UNIT = ((1, 0, 0), (0, 1, 0), (0, 0, 1), (3, 0, 0), (0, 3, 0), (0, 0, 3))
PARENT = (None,) + (0, 0, 0, 2, 1, 3, 6, 4, 4, 5, 5, 7)
DIRS = (
    (None,) + (5, 0, 2, 1, 3, 4, 0, 5, 1, 5, 2, 0),
    (None,) + (4, 3, 1, 2, 0, 5, 3, 4, 2, 4, 1, 3),
)
SLOTS = len(PARENT)
OTHER = 20
MEETINGS = (
    ((0, (0, 20)), (1, (0, 20, 21)), (2, (0, 1, 20, 21)), (3, (1, 2, 20, 21))),
    (
        (4, (0, 1, 2, 3, 21, 22)),
        (5, (2, 3, 4, 20, 21, 23, 24, 25)),
        (6, (0, 1, 4, 5, 20, 22, 23, 25, 26)),
    ),
    (
        (7, (0, 3, 4, 5, 21, 22, 23, 24, 26, 27)),
        (8, (3, 5, 6, 7, 20, 21, 24, 25, 27)),
        (9, (0, 1, 2, 5, 6, 8, 22, 26, 27)),
    ),
    ((10, (2, 9, 20, 21, 23)), (11, (2, 8, 9, 20, 26)), (12, (23, 27))),
)


def members(meeting):
    rows = tuple(k for k, partners in meeting)
    rest = sorted({k for row, partners in meeting for k in partners} - set(rows))
    return rows, rows + tuple(rest)


NAMES = tuple(sorted({k for meeting in MEETINGS for k in members(meeting)[1]}))


def offsets():
    table = []
    for core in range(2):
        held = [(0, 0, 0)]
        for i in range(1, SLOTS):
            step, base = UNIT[DIRS[core][i]], held[PARENT[i]]
            held.append(tuple((a + b) % 4 for a, b in zip(step, base)))
        table.append(held)
    return table


def place(x, y, z, core):
    group = (y // 2) * 4 + x
    row = (z * 2 + y % 2) * 2 + core
    return group * 16 + row


def fetch(block, steps):
    pairs = []
    for x in range(4):
        for y in range(4):
            for z in range(4):
                for core in range(2):
                    dx, dy, dz = steps[core]
                    source = place((x + dx) % 4, (y + dy) % 4, (z + dz) % 4, core)
                    pairs.append((source, place(x, y, z, core)))
    return lax.ppermute(block, AXES, sorted(pairs))


def flip(block):
    return lax.ppermute(block, AXES, [(i, i ^ 1) for i in range(128)])


def home(name, group, row):
    x, y, z = lax.rem(group, 4), lax.div(group, 4) * 2 + lax.rem(lax.div(row, 2), 2), lax.div(row, 4)
    core = lax.rem(row, 2)
    table = offsets()
    swap = 1 if name >= OTHER else 0
    at = []
    for axis, here in enumerate((x, y, z)):
        first = table[swap][name % OTHER][axis]
        second = table[1 - swap][name % OTHER][axis]
        at.append(lax.rem(here + jnp.where(core == 0, first, second), 4))
    core = 1 - core if swap else core
    group = lax.div(at[1], 2) * 4 + at[0]
    return group * 16 + (at[2] * 2 + lax.rem(at[1], 2)) * 2 + core


def prepare_kernel(embeds_ref, member_ref, block_ref, target_ref):
    member = member_ref[...].astype(jnp.float32)
    column = jnp.transpose(jnp.broadcast_to(member, (128, RB)))[:, 0:1]
    above = lax.broadcasted_iota(jnp.int32, (RB, RB), 0)
    across = lax.broadcasted_iota(jnp.int32, (RB, RB), 1)
    before = (column < member) | ((column == member) & (above < across))
    target = jnp.sum(before.astype(jnp.float32), axis=0, keepdims=True).astype(jnp.int32)
    target_ref[...] = target
    values = embeds_ref[...].astype(jnp.float32)
    total = jnp.sum(values * values, axis=1, keepdims=True)
    normed = (values * lax.rsqrt(total + 1e-06)).astype(jnp.bfloat16)
    placer = (above == target).astype(jnp.bfloat16)
    block_ref[0:RB, :] = jnp.dot(placer, normed, preferred_element_type=jnp.float32).astype(
        jnp.bfloat16
    )
    ordered = jnp.sum(jnp.where(above == target, member, 0.0), axis=1, keepdims=True)
    ordered = jnp.transpose(jnp.broadcast_to(ordered, (RB, 128)))[0:META]
    block_ref[RB:SENT, :] = jnp.zeros((META, D), jnp.bfloat16)
    block_ref[RB:SENT, 0:RB] = ordered.astype(jnp.bfloat16)


def prepare(embeds, member):
    return pl.pallas_call(
        prepare_kernel,
        out_shape=(
            jax.ShapeDtypeStruct((SENT, D), jnp.bfloat16),
            jax.ShapeDtypeStruct((1, RB), jnp.int32),
        ),
        name="prepare",
    )(embeds, member.reshape(1, RB))


def meet_kernel(total, rows, pairs, itself, lists, fetched, *refs):
    blocks, refs = refs[:total], refs[total:]
    if lists:
        before, refs = refs[: len(lists) - 1], refs[len(lists) - 1 :]
    out_ref, held, across, down, row_best, column_best, table, waits, sems = refs
    for k in range(total):
        pltpu.make_async_copy(blocks[k], held.at[k], sems.at[k]).start()
    for p, (i, j) in enumerate(pairs):
        table[0, p] = i
        table[1, p] = j
        waits[p] = fetched[p]
    pairs = len(pairs)
    row_best[...] = jnp.full_like(row_best, LOW)
    column_best[...] = jnp.full_like(column_best, LOW)
    if lists:
        out_ref[...] = jnp.full_like(out_ref, ABSENT)

    def arrive(k):
        pltpu.make_async_copy(blocks[0], held.at[k], sems.at[k]).wait()
        across[k] = held[k, RB:SENT, 0:RB].astype(jnp.float32)[0:8]

    for k in range(rows):
        arrive(k)
        down[k] = jnp.transpose(jnp.broadcast_to(across[k, 0:1], (128, RB)))

    def meet(i, j, at, length, column, width, same):
        scores = lax.dot_general(
            held[i, at : at + length, :],
            held[j, column : column + width, :],
            (((1,), (1,)), ((), ())),
            preferred_element_type=jnp.float32,
        )
        here = jnp.concatenate([down[i, at : at + length, :]] * (width // 128), axis=1)
        keep = here == across[j, 0:1, column : column + width]
        if same:
            one = lax.broadcasted_iota(jnp.int32, (length, width), 0)
            keep = keep & (one != lax.broadcasted_iota(jnp.int32, (length, width), 1))
        scores = jnp.where(keep, scores, LOW)
        most = scores[:, 0:128]
        for q in range(1, width // 128):
            most = jnp.maximum(most, scores[:, 128 * q : 128 * q + 128])
        row_best[i, at : at + length, :] = jnp.maximum(row_best[i, at : at + length, :], most)
        top = jnp.max(scores.reshape(length // 8, 8, width), axis=0)
        span = slice(column, column + width)
        column_best[j, :, span] = jnp.maximum(column_best[j, :, span], top)

    def near(i, j):
        meet(i, j, 0, BAND, 0, HALF, False)
        meet(i, j, RB - BAND, BAND, HALF, HALF, False)

    def far(i, j):
        late = across[j, 0:1, HALF - 128 : HALF] >= down[i, BAND : BAND + 1, :]
        early = across[j, 0:1, HALF : HALF + 128] <= down[i, RB - BAND - 1 : RB - BAND, :]
        return jnp.where(late | early, 1.0, 0.0)

    def visit(first, length):
        pairs_here = [(table[0, first + u], table[1, first + u]) for u in range(length)]
        flags = functools.reduce(jnp.maximum, [far(i, j) for i, j in pairs_here])
        flag = jnp.max(flags)
        for i, j in pairs_here:
            near(i, j)

        @pl.when(flag > 0.0)
        def _():
            def rest(p, carry):
                i, j = table[0, p], table[1, p]
                meet(i, j, BAND, RB - BAND, 0, HALF, False)
                meet(i, j, 0, RB - BAND, HALF, HALF, False)
                return carry

            lax.fori_loop(first, first + length, rest, 0)

    if itself:
        meet(0, 0, 0, RB, 0, RB, True)

    def await_step(step, length):
        for u in range(length):
            block = waits[step * UNROLL + u]
            pl.when(block >= 0)(functools.partial(arrive, block))

    def some(step, carry):
        await_step(step, UNROLL)
        visit(step * UNROLL, UNROLL)
        return carry

    steps = pairs // UNROLL
    lax.fori_loop(0, steps, some, 0)
    if pairs > steps * UNROLL:
        await_step(steps, pairs - steps * UNROLL)
        visit(steps * UNROLL, pairs - steps * UNROLL)

    def found_in(k):
        found = jnp.max(column_best[k], axis=0, keepdims=True)
        if k < rows:
            turned = jnp.transpose(row_best[k])
            found = jnp.maximum(found, jnp.max(turned, axis=0, keepdims=True))
        return found

    if not lists:
        for k in range(total):
            out_ref[k : k + 1, :] = found_in(k)
        return
    here = [lax.axis_index(axis) for axis in AXES]
    for name in NAMES:
        found = jnp.full((1, RB), ABSENT, jnp.float32)
        if name in lists[0]:
            found = jnp.maximum(found, found_in(lists[0].index(name)))
        for ref, names in zip(before, lists[1:]):
            if name in names:
                at = names.index(name)
                found = jnp.maximum(found, ref[at : at + 1, :])
        out_ref[home(name, *here)] = found


def meet(held, meeting, lists=(), before=()):
    rows, names = members(meeting)
    pairs = [(i, j) for i, partners in meeting for j in partners]
    itself = (0, 0) in pairs
    pairs = sorted(
        ((names.index(i), names.index(j)) for i, j in pairs if i != j), key=lambda p: p[::-1]
    )
    seen, waits = set(range(len(rows))), []
    for i, j in pairs:
        waits.append(-1 if j in seen else j)
        seen.add(j)
    total = len(names)
    shape = (128, 1, RB) if lists else (total, RB)
    in_specs = [pl.BlockSpec(memory_space=pltpu.HBM)] * total
    if lists:
        in_specs += [pl.BlockSpec(memory_space=pltpu.VMEM)] * len(before)
    return pl.pallas_call(
        functools.partial(meet_kernel, total, len(rows), pairs, itself, lists, waits),
        out_shape=jax.ShapeDtypeStruct(shape, jnp.float32),
        in_specs=in_specs,
        scratch_shapes=[
            pltpu.VMEM((total, SENT, D), jnp.bfloat16),
            pltpu.VMEM((total, 8, RB), jnp.float32),
            pltpu.VMEM((len(rows), RB, 128), jnp.float32),
            pltpu.VMEM((len(rows), RB, 128), jnp.float32),
            pltpu.VMEM((total, 8, RB), jnp.float32),
            pltpu.SMEM((2, len(pairs)), jnp.int32),
            pltpu.SMEM((len(pairs),), jnp.int32),
            pltpu.SemaphoreType.DMA((total,)),
        ],
        compiler_params=pltpu.CompilerParams(vmem_limit_bytes=66_400_000),
        cost_estimate=pl.CostEstimate(
            flops=2 * RB * RB * D * len(pairs),
            bytes_accessed=total * SENT * D * 2,
            transcendentals=0,
        ),
        name=f"meet_{len(pairs)}",
    )(
        *[held[k] for k in names],
        *before,
    )


def finish_kernel(arrived_ref, target_ref, out_ref):
    best = jnp.max(arrived_ref[...], axis=0)
    column = jnp.transpose(jnp.broadcast_to(best, (128, RB)))[:, 0:1]
    above = lax.broadcasted_iota(jnp.int32, (RB, RB), 0)
    picked = jnp.where(above == target_ref[...], column, LOW)
    out_ref[...] = jnp.max(picked, axis=0, keepdims=True)


def finish(arrived, target):
    return pl.pallas_call(
        finish_kernel, out_shape=jax.ShapeDtypeStruct((1, RB), jnp.float32), name="finish"
    )(arrived, target)


def on_device(embeds, member):
    block, target = prepare(embeds, member)
    held = {0: block}
    before = []

    def go(first):
        for i in range(first, first + 3):
            held[i] = fetch(held[PARENT[i]], (UNIT[DIRS[0][i]], UNIT[DIRS[1][i]]))

    def share(slots):
        for i in slots:
            if i + OTHER in NAMES:
                held[i + OTHER] = flip(held[i])

    def after(slots):
        for i in slots:
            before[-1], held[i] = lax.optimization_barrier((before[-1], held[i]))

    go(1)
    share((0, 1, 2, 3))
    go(4)
    before.append(meet(held, MEETINGS[0]))
    after((4, 5, 6))
    go(7)
    share((4, 5, 6))
    before.append(meet(held, MEETINGS[1]))
    after((7, 8, 9))
    go(10)
    share((7, 8, 9))
    before.append(meet(held, MEETINGS[2]))
    lists = tuple(members(meeting)[1] for meeting in (MEETINGS[-1],) + MEETINGS[:-1])
    outgoing = meet(held, MEETINGS[-1], lists, before)
    arrived = lax.all_to_all(outgoing, AXES, split_axis=0, concat_axis=0, tiled=True)
    return finish(arrived, target).reshape(-1)


def solution(mesh):
    in_specs = (P(AXES, None), P(AXES))
    return jax.shard_map(
        on_device, mesh=mesh, in_specs=in_specs, out_specs=P(AXES), check_vma=False
    )
```

```python
import functools

import jax
import jax.numpy as jnp
import numpy as np
from jax import lax
from jax.experimental import pallas as pl
from jax.experimental.pallas import tpu as pltpu
from jax.sharding import PartitionSpec as P

D = 768
RB = 512
GROUPS = 8
META = 16
SENT = RB + META
UNROLL = 4
HALF = 256
BAND = 384
ABSENT = -4.0
LOW = -1e30
AXES = ("group", "row")

UNIT = ((1, 0, 0), (0, 1, 0), (0, 0, 1), (3, 0, 0), (0, 3, 0), (0, 0, 3))
PARENT = (None,) + (0, 0, 0, 0, 2, 1, 4, 2, 5, 7, 9, 5)
DIRS = (
    (None,) + (4, 2, 5, 1, 3, 0, 5, 1, 3, 5, 4, 2),
    (None,) + (1, 3, 0, 4, 2, 5, 0, 4, 2, 0, 1, 3),
)
SLOTS = len(PARENT)
OTHER = 20
MEETINGS = (
    ((0, (0, 20)), (1, (0, 20, 21)), (2, (0, 1, 20, 21, 22)), (3, (1, 2, 20, 21, 22, 23))),
    (
        (4, (1, 20, 23)),
        (5, (0, 1, 2, 3, 4, 21, 23, 24)),
        (6, (0, 3, 4, 5, 21, 22, 26)),
    ),
    (
        (7, (1, 2, 5, 6, 23, 24, 27)),
        (8, (5, 6, 20, 22, 27)),
        (9, (0, 2, 3, 4, 6, 21, 24, 26)),
    ),
    (
        (10, (1, 6, 20, 21, 23, 24, 27)),
        (11, (2, 6, 7, 8, 10, 21, 23, 26)),
        (12, (1, 6, 20, 21, 23, 26, 27)),
    ),
)


def members(meeting):
    rows = tuple(k for k, partners in meeting)
    rest = sorted({k for row, partners in meeting for k in partners} - set(rows))
    return rows, rows + tuple(rest)


NAMES = tuple(sorted({k for meeting in MEETINGS for k in members(meeting)[1]}))


def offsets():
    table = []
    for core in range(2):
        held = [(0, 0, 0)]
        for i in range(1, SLOTS):
            step, base = UNIT[DIRS[core][i]], held[PARENT[i]]
            held.append(tuple((a + b) % 4 for a, b in zip(step, base)))
        table.append(held)
    return table


def place(x, y, z, core):
    group = (y // 2) * 4 + x
    row = (z * 2 + y % 2) * 2 + core
    return group * 16 + row


def fetch(block, steps):
    pairs = []
    for x in range(4):
        for y in range(4):
            for z in range(4):
                for core in range(2):
                    dx, dy, dz = steps[core]
                    source = place((x + dx) % 4, (y + dy) % 4, (z + dz) % 4, core)
                    pairs.append((source, place(x, y, z, core)))
    return lax.ppermute(block, AXES, sorted(pairs))


def flip(block):
    return lax.ppermute(block, AXES, [(i, i ^ 1) for i in range(128)])


def home(name, group, row):
    x, y, z = lax.rem(group, 4), lax.div(group, 4) * 2 + lax.rem(lax.div(row, 2), 2), lax.div(row, 4)
    core = lax.rem(row, 2)
    table = offsets()
    swap = 1 if name >= OTHER else 0
    at = []
    for axis, here in enumerate((x, y, z)):
        first = table[swap][name % OTHER][axis]
        second = table[1 - swap][name % OTHER][axis]
        at.append(lax.rem(here + jnp.where(core == 0, first, second), 4))
    core = 1 - core if swap else core
    group = lax.div(at[1], 2) * 4 + at[0]
    return group * 16 + (at[2] * 2 + lax.rem(at[1], 2)) * 2 + core


def prepare_kernel(embeds_ref, member_ref, block_ref, target_ref):
    member = member_ref[...].astype(jnp.float32)
    cluster = lax.broadcasted_iota(jnp.int32, (16, RB), 0).astype(jnp.float32)
    hits = cluster == member
    ones = jnp.where(hits, 1.0, 0.0)
    above = lax.broadcasted_iota(jnp.int32, (RB, RB), 0)
    across = lax.broadcasted_iota(jnp.int32, (RB, RB), 1)
    earlier = (above < across).astype(jnp.bfloat16)
    rank = jnp.dot(ones.astype(jnp.bfloat16), earlier, preferred_element_type=jnp.float32)
    counts = jnp.sum(ones, axis=1, keepdims=True)
    parts = jnp.where(cluster < member, counts, 0.0) + jnp.where(hits, rank, 0.0)
    target = jnp.sum(parts, axis=0, keepdims=True).astype(jnp.int32)
    target_ref[...] = target
    values = embeds_ref[...].astype(jnp.float32)
    total = jnp.sum(values * values, axis=1, keepdims=True)
    normed = (values * lax.rsqrt(total + 1e-06)).astype(jnp.bfloat16)
    placer = (above == target).astype(jnp.bfloat16)
    block_ref[0:RB, :] = jnp.dot(placer, normed, preferred_element_type=jnp.float32).astype(
        jnp.bfloat16
    )
    upto = lax.broadcasted_iota(jnp.int32, (16, 16), 1) <= lax.broadcasted_iota(
        jnp.int32, (16, 16), 0
    )
    spread = jnp.transpose(jnp.broadcast_to(counts, (16, 16)))
    ends = jnp.sum(jnp.where(upto, spread, 0.0), axis=1, keepdims=True)
    places = lax.broadcasted_iota(jnp.int32, (16, RB), 1).astype(jnp.float32)
    passed = jnp.where(places >= ends, 1.0, 0.0)[0:GROUPS]
    ordered = jnp.sum(passed, axis=0, keepdims=True)
    block_ref[RB:SENT, :] = jnp.zeros((META, D), jnp.bfloat16)
    block_ref[RB:SENT, 0:RB] = jnp.broadcast_to(ordered, (META, RB)).astype(jnp.bfloat16)


def prepare(embeds, member):
    return pl.pallas_call(
        prepare_kernel,
        out_shape=(
            jax.ShapeDtypeStruct((SENT, D), jnp.bfloat16),
            jax.ShapeDtypeStruct((1, RB), jnp.int32),
        ),
        name="prepare",
    )(embeds, member.reshape(1, RB))


def meet_kernel(total, rows, pairs, itself, lists, fetched, *refs):
    blocks, refs = refs[:total], refs[total:]
    if lists:
        before, refs = refs[: len(lists) - 1], refs[len(lists) - 1 :]
    out_ref, held, across, down, row_best, column_best, table, waits, sems = refs
    for k in range(total):
        pltpu.make_async_copy(blocks[k], held.at[k], sems.at[k]).start()
    for p, (i, j) in enumerate(pairs):
        table[0, p] = i
        table[1, p] = j
        waits[p] = fetched[p]
    pairs = len(pairs)
    row_best[...] = jnp.full_like(row_best, LOW)
    column_best[...] = jnp.full_like(column_best, LOW)
    if lists:
        out_ref[...] = jnp.full_like(out_ref, ABSENT)

    def arrive(k):
        pltpu.make_async_copy(blocks[0], held.at[k], sems.at[k]).wait()
        across[k] = held[k, RB:SENT, 0:RB].astype(jnp.float32)[0:8]

    for k in range(rows):
        arrive(k)
        down[k] = jnp.transpose(jnp.broadcast_to(across[k, 0:1], (128, RB)))

    def meet(i, j, at, length, column, width, same):
        scores = lax.dot_general(
            held[i, at : at + length, :],
            held[j, column : column + width, :],
            (((1,), (1,)), ((), ())),
            preferred_element_type=jnp.float32,
        )
        here = jnp.concatenate([down[i, at : at + length, :]] * (width // 128), axis=1)
        keep = here == across[j, 0:1, column : column + width]
        if same:
            one = lax.broadcasted_iota(jnp.int32, (length, width), 0)
            keep = keep & (one != lax.broadcasted_iota(jnp.int32, (length, width), 1))
        scores = jnp.where(keep, scores, LOW)
        most = scores[:, 0:128]
        for q in range(1, width // 128):
            most = jnp.maximum(most, scores[:, 128 * q : 128 * q + 128])
        row_best[i, at : at + length, :] = jnp.maximum(row_best[i, at : at + length, :], most)
        top = jnp.max(scores.reshape(length // 8, 8, width), axis=0)
        span = slice(column, column + width)
        column_best[j, :, span] = jnp.maximum(column_best[j, :, span], top)

    def near(i, j):
        meet(i, j, 0, BAND, 0, HALF, False)
        meet(i, j, RB - BAND, BAND, HALF, HALF, False)

    def far(i, j):
        late = across[j, 0:1, HALF - 128 : HALF] >= down[i, BAND : BAND + 1, :]
        early = across[j, 0:1, HALF : HALF + 128] <= down[i, RB - BAND - 1 : RB - BAND, :]
        return jnp.where(late | early, 1.0, 0.0)

    def visit(first, length):
        pairs_here = [(table[0, first + u], table[1, first + u]) for u in range(length)]
        flags = functools.reduce(jnp.maximum, [far(i, j) for i, j in pairs_here])
        flag = jnp.max(flags)
        for i, j in pairs_here:
            near(i, j)

        @pl.when(flag > 0.0)
        def _():
            def rest(p, carry):
                i, j = table[0, p], table[1, p]
                meet(i, j, BAND, RB - BAND, 0, HALF, False)
                meet(i, j, 0, RB - BAND, HALF, HALF, False)
                return carry

            lax.fori_loop(first, first + length, rest, 0)

    if itself:
        meet(0, 0, 0, RB, 0, RB, True)

    def await_step(step, length):
        for u in range(length):
            block = waits[step * UNROLL + u]
            pl.when(block >= 0)(functools.partial(arrive, block))

    def some(step, carry):
        await_step(step, UNROLL)
        visit(step * UNROLL, UNROLL)
        return carry

    steps = pairs // UNROLL
    lax.fori_loop(0, steps, some, 0)
    if pairs > steps * UNROLL:
        await_step(steps, pairs - steps * UNROLL)
        visit(steps * UNROLL, pairs - steps * UNROLL)

    def found_in(k):
        found = jnp.max(column_best[k], axis=0, keepdims=True)
        if k < rows:
            turned = jnp.transpose(row_best[k])
            found = jnp.maximum(found, jnp.max(turned, axis=0, keepdims=True))
        return found

    if not lists:
        for k in range(total):
            out_ref[k : k + 1, :] = found_in(k)
        return
    here = [lax.axis_index(axis) for axis in AXES]
    for name in NAMES:
        found = jnp.full((1, RB), ABSENT, jnp.float32)
        if name in lists[0]:
            found = jnp.maximum(found, found_in(lists[0].index(name)))
        for ref, names in zip(before, lists[1:]):
            if name in names:
                at = names.index(name)
                found = jnp.maximum(found, ref[at : at + 1, :])
        out_ref[home(name, *here)] = found


def meet(held, meeting, lists=(), before=()):
    rows, names = members(meeting)
    pairs = [(i, j) for i, partners in meeting for j in partners]
    itself = (0, 0) in pairs
    pairs = sorted(
        ((names.index(i), names.index(j)) for i, j in pairs if i != j), key=lambda p: p[::-1]
    )
    seen, waits = set(range(len(rows))), []
    for i, j in pairs:
        waits.append(-1 if j in seen else j)
        seen.add(j)
    total = len(names)
    shape = (128, 1, RB) if lists else (total, RB)
    in_specs = [pl.BlockSpec(memory_space=pltpu.HBM)] * total
    if lists:
        in_specs += [pl.BlockSpec(memory_space=pltpu.VMEM)] * len(before)
    return pl.pallas_call(
        functools.partial(meet_kernel, total, len(rows), pairs, itself, lists, waits),
        out_shape=jax.ShapeDtypeStruct(shape, jnp.float32),
        in_specs=in_specs,
        scratch_shapes=[
            pltpu.VMEM((total, SENT, D), jnp.bfloat16),
            pltpu.VMEM((total, 8, RB), jnp.float32),
            pltpu.VMEM((len(rows), RB, 128), jnp.float32),
            pltpu.VMEM((len(rows), RB, 128), jnp.float32),
            pltpu.VMEM((total, 8, RB), jnp.float32),
            pltpu.SMEM((2, len(pairs)), jnp.int32),
            pltpu.SMEM((len(pairs),), jnp.int32),
            pltpu.SemaphoreType.DMA((total,)),
        ],
        compiler_params=pltpu.CompilerParams(vmem_limit_bytes=66_400_000),
        cost_estimate=pl.CostEstimate(
            flops=2 * RB * RB * D * len(pairs),
            bytes_accessed=total * SENT * D * 2,
            transcendentals=0,
        ),
        name=f"meet_{len(pairs)}",
    )(
        *[held[k] for k in names],
        *before,
    )


def finish_kernel(arrived_ref, target_ref, out_ref):
    best = jnp.max(arrived_ref[...], axis=0)
    column = jnp.transpose(jnp.broadcast_to(best, (128, RB)))[:, 0:1]
    above = lax.broadcasted_iota(jnp.int32, (RB, RB), 0)
    picked = jnp.where(above == target_ref[...], column, LOW)
    out_ref[...] = jnp.max(picked, axis=0, keepdims=True)


def finish(arrived, target):
    return pl.pallas_call(
        finish_kernel, out_shape=jax.ShapeDtypeStruct((1, RB), jnp.float32), name="finish"
    )(arrived, target)


def on_device(embeds, member):
    block, target = prepare(embeds, member)
    held = {0: block}
    before = []

    def go(first):
        for i in range(first, first + 3):
            held[i] = fetch(held[PARENT[i]], (UNIT[DIRS[0][i]], UNIT[DIRS[1][i]]))

    def share(slots):
        for i in slots:
            if i + OTHER in NAMES:
                held[i + OTHER] = flip(held[i])

    def after(slots):
        for i in slots:
            before[-1], held[i] = lax.optimization_barrier((before[-1], held[i]))

    go(1)
    share((0, 1, 2, 3))
    go(4)
    before.append(meet(held, MEETINGS[0]))
    after((4, 5, 6))
    go(7)
    share((4, 5, 6))
    before.append(meet(held, MEETINGS[1]))
    after((7, 8, 9))
    go(10)
    share((7, 8, 9))
    before.append(meet(held, MEETINGS[2]))
    lists = tuple(members(meeting)[1] for meeting in (MEETINGS[-1],) + MEETINGS[:-1])
    outgoing = meet(held, MEETINGS[-1], lists, before)
    arrived = lax.all_to_all(outgoing, AXES, split_axis=0, concat_axis=0, tiled=True)
    return finish(arrived, target).reshape(-1)


def solution(mesh):
    in_specs = (P(AXES, None), P(AXES))
    return jax.shard_map(
        on_device, mesh=mesh, in_specs=in_specs, out_specs=P(AXES), check_vma=False
    )
```

```python
import functools

import jax
import jax.numpy as jnp
import numpy as np
from jax import lax
from jax.experimental import pallas as pl
from jax.experimental.pallas import tpu as pltpu
from jax.sharding import PartitionSpec as P

D = 768
RB = 512
GROUPS = 8
META = 16
SENT = RB + META
UNROLL = 4
HALF = 256
BAND = 384
ABSENT = -4.0
LOW = -1e30
AXES = ("group", "row")

UNIT = ((1, 0, 0), (0, 1, 0), (0, 0, 1), (3, 0, 0), (0, 3, 0), (0, 0, 3))
PARENT = (None,) + (0, 0, 0, 2, 1, 3, 6, 4, 4, 5, 5, 7)
DIRS = (
    (None,) + (5, 0, 2, 1, 3, 4, 0, 5, 1, 5, 2, 0),
    (None,) + (4, 3, 1, 2, 0, 5, 3, 4, 2, 4, 1, 3),
)
SLOTS = len(PARENT)
OTHER = 20
MEETINGS = (
    ((0, (0, 20)), (1, (0, 20, 21)), (2, (0, 1, 20, 21)), (3, (1, 2, 20, 21))),
    (
        (4, (0, 1, 2, 3, 21, 22)),
        (5, (2, 3, 4, 20, 21, 23, 24, 25)),
        (6, (0, 1, 4, 5, 20, 22, 23, 25, 26)),
    ),
    (
        (7, (0, 3, 4, 5, 21, 22, 23, 24, 26, 27)),
        (8, (3, 5, 6, 7, 20, 21, 24, 25, 27)),
        (9, (0, 1, 2, 5, 6, 8, 22, 26, 27)),
    ),
    ((10, (2, 9, 20, 21, 23)), (11, (2, 8, 9, 20, 26)), (12, (23, 27))),
)


def members(meeting):
    rows = tuple(k for k, partners in meeting)
    rest = sorted({k for row, partners in meeting for k in partners} - set(rows))
    return rows, rows + tuple(rest)


NAMES = tuple(sorted({k for meeting in MEETINGS for k in members(meeting)[1]}))


def offsets():
    table = []
    for core in range(2):
        held = [(0, 0, 0)]
        for i in range(1, SLOTS):
            step, base = UNIT[DIRS[core][i]], held[PARENT[i]]
            held.append(tuple((a + b) % 4 for a, b in zip(step, base)))
        table.append(held)
    return table


def place(x, y, z, core):
    group = (y // 2) * 4 + x
    row = (z * 2 + y % 2) * 2 + core
    return group * 16 + row


def fetch(block, steps):
    pairs = []
    for x in range(4):
        for y in range(4):
            for z in range(4):
                for core in range(2):
                    dx, dy, dz = steps[core]
                    source = place((x + dx) % 4, (y + dy) % 4, (z + dz) % 4, core)
                    pairs.append((source, place(x, y, z, core)))
    return lax.ppermute(block, AXES, sorted(pairs))


def flip(block):
    return lax.ppermute(block, AXES, [(i, i ^ 1) for i in range(128)])


def home(name, group, row):
    x, y, z = lax.rem(group, 4), lax.div(group, 4) * 2 + lax.rem(lax.div(row, 2), 2), lax.div(row, 4)
    core = lax.rem(row, 2)
    table = offsets()
    swap = 1 if name >= OTHER else 0
    at = []
    for axis, here in enumerate((x, y, z)):
        first = table[swap][name % OTHER][axis]
        second = table[1 - swap][name % OTHER][axis]
        at.append(lax.rem(here + jnp.where(core == 0, first, second), 4))
    core = 1 - core if swap else core
    group = lax.div(at[1], 2) * 4 + at[0]
    return group * 16 + (at[2] * 2 + lax.rem(at[1], 2)) * 2 + core


def prepare_kernel(embeds_ref, member_ref, block_ref, target_ref):
    member = member_ref[...].astype(jnp.float32)
    cluster = lax.broadcasted_iota(jnp.int32, (16, RB), 0).astype(jnp.float32)
    hits = cluster == member
    ones = jnp.where(hits, 1.0, 0.0)
    above = lax.broadcasted_iota(jnp.int32, (RB, RB), 0)
    across = lax.broadcasted_iota(jnp.int32, (RB, RB), 1)
    earlier = (above < across).astype(jnp.bfloat16)
    rank = jnp.dot(ones.astype(jnp.bfloat16), earlier, preferred_element_type=jnp.float32)
    counts = jnp.sum(ones, axis=1, keepdims=True)
    parts = jnp.where(cluster < member, counts, 0.0) + jnp.where(hits, rank, 0.0)
    target = jnp.sum(parts, axis=0, keepdims=True).astype(jnp.int32)
    target_ref[...] = target
    values = embeds_ref[...].astype(jnp.float32)
    total = jnp.sum(values * values, axis=1, keepdims=True)
    normed = (values * lax.rsqrt(total + 1e-06)).astype(jnp.bfloat16)
    placer = (above == target).astype(jnp.bfloat16)
    block_ref[0:RB, :] = jnp.dot(placer, normed, preferred_element_type=jnp.float32).astype(
        jnp.bfloat16
    )
    upto = lax.broadcasted_iota(jnp.int32, (16, 16), 1) <= lax.broadcasted_iota(
        jnp.int32, (16, 16), 0
    )
    spread = jnp.transpose(jnp.broadcast_to(counts, (16, 16)))
    ends = jnp.sum(jnp.where(upto, spread, 0.0), axis=1, keepdims=True)
    places = lax.broadcasted_iota(jnp.int32, (16, RB), 1).astype(jnp.float32)
    passed = jnp.where(places >= ends, 1.0, 0.0)[0:GROUPS]
    ordered = jnp.sum(passed, axis=0, keepdims=True)
    block_ref[RB:SENT, :] = jnp.zeros((META, D), jnp.bfloat16)
    block_ref[RB:SENT, 0:RB] = jnp.broadcast_to(ordered, (META, RB)).astype(jnp.bfloat16)


def prepare(embeds, member):
    return pl.pallas_call(
        prepare_kernel,
        out_shape=(
            jax.ShapeDtypeStruct((SENT, D), jnp.bfloat16),
            jax.ShapeDtypeStruct((1, RB), jnp.int32),
        ),
        name="prepare",
    )(embeds, member.reshape(1, RB))


def meet_kernel(total, rows, pairs, itself, lists, fetched, *refs):
    blocks, refs = refs[:total], refs[total:]
    if lists:
        before, refs = refs[: len(lists) - 1], refs[len(lists) - 1 :]
    out_ref, held, across, down, row_best, column_best, table, waits, sems = refs
    for k in range(total):
        pltpu.make_async_copy(blocks[k], held.at[k], sems.at[k]).start()
    for p, (i, j) in enumerate(pairs):
        table[0, p] = i
        table[1, p] = j
        waits[p] = fetched[p]
    pairs = len(pairs)
    row_best[...] = jnp.full_like(row_best, LOW)
    column_best[...] = jnp.full_like(column_best, LOW)
    if lists:
        out_ref[...] = jnp.full_like(out_ref, ABSENT)

    def arrive(k):
        pltpu.make_async_copy(blocks[0], held.at[k], sems.at[k]).wait()
        across[k] = held[k, RB:SENT, 0:RB].astype(jnp.float32)[0:8]

    for k in range(rows):
        arrive(k)
        down[k] = jnp.transpose(jnp.broadcast_to(across[k, 0:1], (128, RB)))

    def meet(i, j, at, length, column, width, same):
        scores = lax.dot_general(
            held[i, at : at + length, :],
            held[j, column : column + width, :],
            (((1,), (1,)), ((), ())),
            preferred_element_type=jnp.float32,
        )
        here = jnp.concatenate([down[i, at : at + length, :]] * (width // 128), axis=1)
        keep = here == across[j, 0:1, column : column + width]
        if same:
            one = lax.broadcasted_iota(jnp.int32, (length, width), 0)
            keep = keep & (one != lax.broadcasted_iota(jnp.int32, (length, width), 1))
        scores = jnp.where(keep, scores, LOW)
        most = scores[:, 0:128]
        for q in range(1, width // 128):
            most = jnp.maximum(most, scores[:, 128 * q : 128 * q + 128])
        row_best[i, at : at + length, :] = jnp.maximum(row_best[i, at : at + length, :], most)
        top = jnp.max(scores.reshape(length // 8, 8, width), axis=0)
        span = slice(column, column + width)
        column_best[j, :, span] = jnp.maximum(column_best[j, :, span], top)

    def near(i, j):
        meet(i, j, 0, BAND, 0, HALF, False)
        meet(i, j, RB - BAND, BAND, HALF, HALF, False)

    def far(i, j):
        below = across[j, 0:1, HALF - 128 : HALF] >= down[i, BAND : BAND + 1, :]
        above = across[j, 0:1, HALF : HALF + 128] <= down[i, RB - BAND - 1 : RB - BAND, :]
        return jnp.where(below, 1.0, 0.0), jnp.where(above, 1.0, 0.0)

    def visit(first, length):
        pairs_here = [(table[0, first + u], table[1, first + u]) for u in range(length)]
        flags = [jnp.maximum(*far(i, j)) for i, j in pairs_here]
        flag = jnp.max(functools.reduce(jnp.maximum, flags))
        for i, j in pairs_here:
            near(i, j)

        @pl.when(flag > 0.0)
        def _():
            def rest(p, carry):
                i, j = table[0, p], table[1, p]
                below, above = (jnp.max(lanes) for lanes in far(i, j))

                @pl.when(below > 0.0)
                def _():
                    meet(i, j, BAND, RB - BAND, 0, HALF, False)

                @pl.when(above > 0.0)
                def _():
                    meet(i, j, 0, RB - BAND, HALF, HALF, False)

                return carry

            lax.fori_loop(first, first + length, rest, 0)

    if itself:
        meet(0, 0, 0, RB, 0, RB, True)

    def await_step(step, length):
        for u in range(length):
            block = waits[step * UNROLL + u]
            pl.when(block >= 0)(functools.partial(arrive, block))

    def some(step, carry):
        await_step(step, UNROLL)
        visit(step * UNROLL, UNROLL)
        return carry

    steps = pairs // UNROLL
    lax.fori_loop(0, steps, some, 0)
    if pairs > steps * UNROLL:
        await_step(steps, pairs - steps * UNROLL)
        visit(steps * UNROLL, pairs - steps * UNROLL)

    def found_in(k):
        found = jnp.max(column_best[k], axis=0, keepdims=True)
        if k < rows:
            turned = jnp.transpose(row_best[k])
            found = jnp.maximum(found, jnp.max(turned, axis=0, keepdims=True))
        return found

    if not lists:
        for k in range(total):
            out_ref[k : k + 1, :] = found_in(k)
        return
    here = [lax.axis_index(axis) for axis in AXES]
    for name in NAMES:
        found = jnp.full((1, RB), ABSENT, jnp.float32)
        if name in lists[0]:
            found = jnp.maximum(found, found_in(lists[0].index(name)))
        for ref, names in zip(before, lists[1:]):
            if name in names:
                at = names.index(name)
                found = jnp.maximum(found, ref[at : at + 1, :])
        out_ref[home(name, *here)] = found


def meet(held, meeting, lists=(), before=()):
    rows, names = members(meeting)
    pairs = [(i, j) for i, partners in meeting for j in partners]
    itself = (0, 0) in pairs
    pairs = sorted(
        ((names.index(i), names.index(j)) for i, j in pairs if i != j), key=lambda p: p[::-1]
    )
    seen, waits = set(range(len(rows))), []
    for i, j in pairs:
        waits.append(-1 if j in seen else j)
        seen.add(j)
    total = len(names)
    shape = (128, 1, RB) if lists else (total, RB)
    in_specs = [pl.BlockSpec(memory_space=pltpu.HBM)] * total
    if lists:
        in_specs += [pl.BlockSpec(memory_space=pltpu.VMEM)] * len(before)
    return pl.pallas_call(
        functools.partial(meet_kernel, total, len(rows), pairs, itself, lists, waits),
        out_shape=jax.ShapeDtypeStruct(shape, jnp.float32),
        in_specs=in_specs,
        scratch_shapes=[
            pltpu.VMEM((total, SENT, D), jnp.bfloat16),
            pltpu.VMEM((total, 8, RB), jnp.float32),
            pltpu.VMEM((len(rows), RB, 128), jnp.float32),
            pltpu.VMEM((len(rows), RB, 128), jnp.float32),
            pltpu.VMEM((total, 8, RB), jnp.float32),
            pltpu.SMEM((2, len(pairs)), jnp.int32),
            pltpu.SMEM((len(pairs),), jnp.int32),
            pltpu.SemaphoreType.DMA((total,)),
        ],
        compiler_params=pltpu.CompilerParams(vmem_limit_bytes=66_400_000),
        cost_estimate=pl.CostEstimate(
            flops=2 * RB * RB * D * len(pairs),
            bytes_accessed=total * SENT * D * 2,
            transcendentals=0,
        ),
        name=f"meet_{len(pairs)}",
    )(
        *[held[k] for k in names],
        *before,
    )


def finish_kernel(arrived_ref, target_ref, out_ref):
    best = jnp.max(arrived_ref[...], axis=0)
    column = jnp.transpose(jnp.broadcast_to(best, (128, RB)))[:, 0:1]
    above = lax.broadcasted_iota(jnp.int32, (RB, RB), 0)
    picked = jnp.where(above == target_ref[...], column, LOW)
    out_ref[...] = jnp.max(picked, axis=0, keepdims=True)


def finish(arrived, target):
    return pl.pallas_call(
        finish_kernel, out_shape=jax.ShapeDtypeStruct((1, RB), jnp.float32), name="finish"
    )(arrived, target)


def on_device(embeds, member):
    block, target = prepare(embeds, member)
    held = {0: block}
    before = []

    def go(first):
        for i in range(first, first + 3):
            held[i] = fetch(held[PARENT[i]], (UNIT[DIRS[0][i]], UNIT[DIRS[1][i]]))

    def share(slots):
        for i in slots:
            if i + OTHER in NAMES:
                held[i + OTHER] = flip(held[i])

    def after(slots):
        for i in slots:
            before[-1], held[i] = lax.optimization_barrier((before[-1], held[i]))

    go(1)
    share((0, 1, 2, 3))
    go(4)
    before.append(meet(held, MEETINGS[0]))
    after((4, 5, 6))
    go(7)
    share((4, 5, 6))
    before.append(meet(held, MEETINGS[1]))
    after((7, 8, 9))
    go(10)
    share((7, 8, 9))
    before.append(meet(held, MEETINGS[2]))
    lists = tuple(members(meeting)[1] for meeting in (MEETINGS[-1],) + MEETINGS[:-1])
    outgoing = meet(held, MEETINGS[-1], lists, before)
    arrived = lax.all_to_all(outgoing, AXES, split_axis=0, concat_axis=0, tiled=True)
    return finish(arrived, target).reshape(-1)


def solution(mesh):
    in_specs = (P(AXES, None), P(AXES))
    return jax.shard_map(
        on_device, mesh=mesh, in_specs=in_specs, out_specs=P(AXES), check_vma=False
    )
```

```python
import functools

import jax
import jax.numpy as jnp
import numpy as np
from jax import lax
from jax.experimental import pallas as pl
from jax.experimental.pallas import tpu as pltpu
from jax.sharding import PartitionSpec as P

D = 768
RB = 512
GROUPS = 8
META = 16
SENT = RB + META
UNROLL = 4
HALF = 256
BAND = 384
ABSENT = -4.0
LOW = -1e30
AXES = ("group", "row")

UNIT = ((1, 0, 0), (0, 1, 0), (0, 0, 1), (3, 0, 0), (0, 3, 0), (0, 0, 3))
PARENT = (None,) + (0, 0, 0, 2, 1, 3, 6, 4, 4, 5, 5, 7)
DIRS = (
    (None,) + (5, 0, 2, 1, 3, 4, 0, 5, 1, 5, 2, 0),
    (None,) + (4, 3, 1, 2, 0, 5, 3, 4, 2, 4, 1, 3),
)
SLOTS = len(PARENT)
OTHER = 20
MEETINGS = (
    ((0, (0, 20)), (1, (0, 20, 21)), (2, (0, 1, 20, 21)), (3, (1, 2, 20, 21))),
    (
        (4, (0, 1, 2, 3, 21, 22)),
        (5, (2, 3, 4, 20, 21, 23, 24, 25)),
        (6, (0, 1, 4, 5, 20, 22, 23, 25, 26)),
    ),
    (
        (7, (0, 3, 4, 5, 21, 22, 23, 24, 26, 27)),
        (8, (3, 5, 6, 7, 20, 21, 24, 25, 27)),
        (9, (0, 1, 2, 5, 6, 8, 22, 26, 27)),
    ),
    ((10, (2, 9, 20, 21, 23)), (11, (2, 8, 9, 20, 26)), (12, (23, 27))),
)


def members(meeting):
    rows = tuple(k for k, partners in meeting)
    rest = sorted({k for row, partners in meeting for k in partners} - set(rows))
    return rows, rows + tuple(rest)


NAMES = tuple(sorted({k for meeting in MEETINGS for k in members(meeting)[1]}))


def offsets():
    table = []
    for core in range(2):
        held = [(0, 0, 0)]
        for i in range(1, SLOTS):
            step, base = UNIT[DIRS[core][i]], held[PARENT[i]]
            held.append(tuple((a + b) % 4 for a, b in zip(step, base)))
        table.append(held)
    return table


def place(x, y, z, core):
    group = (y // 2) * 4 + x
    row = (z * 2 + y % 2) * 2 + core
    return group * 16 + row


def fetch(block, steps):
    pairs = []
    for x in range(4):
        for y in range(4):
            for z in range(4):
                for core in range(2):
                    dx, dy, dz = steps[core]
                    source = place((x + dx) % 4, (y + dy) % 4, (z + dz) % 4, core)
                    pairs.append((source, place(x, y, z, core)))
    return lax.ppermute(block, AXES, sorted(pairs))


def flip(block):
    return lax.ppermute(block, AXES, [(i, i ^ 1) for i in range(128)])


def home(name, group, row):
    x, y, z, core = group & 3, ((group >> 2) << 1) | ((row >> 1) & 1), row >> 2, row & 1
    table = offsets()
    swap = 1 if name >= OTHER else 0
    at = []
    for axis, here in enumerate((x, y, z)):
        first = table[swap][name % OTHER][axis]
        second = table[1 - swap][name % OTHER][axis]
        at.append((here + first + core * (second - first)) & 3)
    group = ((at[1] >> 1) << 2) | at[0]
    return (group << 4) | (at[2] << 2) | ((at[1] & 1) << 1) | (core ^ swap)


def prepare_kernel(embeds_ref, member_ref, block_ref, target_ref):
    member = member_ref[...].astype(jnp.float32)
    cluster = lax.broadcasted_iota(jnp.int32, (16, RB), 0).astype(jnp.float32)
    hits = cluster == member
    ones = jnp.where(hits, 1.0, 0.0)
    above = lax.broadcasted_iota(jnp.int32, (RB, RB), 0)
    across = lax.broadcasted_iota(jnp.int32, (RB, RB), 1)
    earlier = (above < across).astype(jnp.bfloat16)
    rank = jnp.dot(ones.astype(jnp.bfloat16), earlier, preferred_element_type=jnp.float32)
    counts = jnp.sum(ones, axis=1, keepdims=True)
    parts = jnp.where(cluster < member, counts, 0.0) + jnp.where(hits, rank, 0.0)
    target = jnp.sum(parts, axis=0, keepdims=True).astype(jnp.int32)
    target_ref[...] = target
    values = embeds_ref[...].astype(jnp.float32)
    total = jnp.sum(values * values, axis=1, keepdims=True)
    normed = (values * lax.rsqrt(total + 1e-06)).astype(jnp.bfloat16)
    placer = (above == target).astype(jnp.bfloat16)
    block_ref[0:RB, :] = jnp.dot(placer, normed, preferred_element_type=jnp.float32).astype(
        jnp.bfloat16
    )
    upto = lax.broadcasted_iota(jnp.int32, (16, 16), 1) <= lax.broadcasted_iota(
        jnp.int32, (16, 16), 0
    )
    spread = jnp.transpose(jnp.broadcast_to(counts, (16, 16)))
    ends = jnp.sum(jnp.where(upto, spread, 0.0), axis=1, keepdims=True)
    places = lax.broadcasted_iota(jnp.int32, (16, RB), 1).astype(jnp.float32)
    passed = jnp.where(places >= ends, 1.0, 0.0)[0:GROUPS]
    ordered = jnp.sum(passed, axis=0, keepdims=True)
    block_ref[RB:SENT, :] = jnp.zeros((META, D), jnp.bfloat16)
    block_ref[RB:SENT, 0:RB] = jnp.broadcast_to(ordered, (META, RB)).astype(jnp.bfloat16)


def prepare(embeds, member):
    return pl.pallas_call(
        prepare_kernel,
        out_shape=(
            jax.ShapeDtypeStruct((SENT, D), jnp.bfloat16),
            jax.ShapeDtypeStruct((1, RB), jnp.int32),
        ),
        name="prepare",
    )(embeds, member.reshape(1, RB))


def meet_kernel(total, rows, pairs, itself, lists, fetched, *refs):
    blocks, refs = refs[:total], refs[total:]
    if lists:
        before, refs = refs[: len(lists) - 1], refs[len(lists) - 1 :]
    out_ref, held, across, down, row_best, column_best, table, waits, sems = refs
    for k in range(total):
        pltpu.make_async_copy(blocks[k], held.at[k], sems.at[k]).start()
    for p, (i, j) in enumerate(pairs):
        table[0, p] = i
        table[1, p] = j
        waits[p] = fetched[p]
    pairs = len(pairs)
    row_best[...] = jnp.full_like(row_best, LOW)
    column_best[...] = jnp.full_like(column_best, LOW)
    if lists:
        out_ref[...] = jnp.full_like(out_ref, ABSENT)
        here = [lax.axis_index(axis) for axis in AXES]
        homes = {name: home(name, *here) for name in NAMES}

        def found_before(name):
            found = jnp.full((1, RB), ABSENT, jnp.float32)
            for ref, names in zip(before, lists[1:]):
                if name in names:
                    at = names.index(name)
                    found = jnp.maximum(found, ref[at : at + 1, :])
            return found

        for name in NAMES:
            if name not in lists[0]:
                out_ref[homes[name]] = found_before(name)

    def arrive(k):
        pltpu.make_async_copy(blocks[0], held.at[k], sems.at[k]).wait()
        across[k] = held[k, RB:SENT, 0:RB].astype(jnp.float32)[0:8]

    for k in range(rows):
        arrive(k)
        down[k] = jnp.transpose(jnp.broadcast_to(across[k, 0:1], (128, RB)))

    def meet(i, j, at, length, column, width, same):
        scores = lax.dot_general(
            held[i, at : at + length, :],
            held[j, column : column + width, :],
            (((1,), (1,)), ((), ())),
            preferred_element_type=jnp.float32,
        )
        here = jnp.concatenate([down[i, at : at + length, :]] * (width // 128), axis=1)
        keep = here == across[j, 0:1, column : column + width]
        if same:
            one = lax.broadcasted_iota(jnp.int32, (length, width), 0)
            keep = keep & (one != lax.broadcasted_iota(jnp.int32, (length, width), 1))
        scores = jnp.where(keep, scores, LOW)
        most = scores[:, 0:128]
        for q in range(1, width // 128):
            most = jnp.maximum(most, scores[:, 128 * q : 128 * q + 128])
        row_best[i, at : at + length, :] = jnp.maximum(row_best[i, at : at + length, :], most)
        top = jnp.max(scores.reshape(length // 8, 8, width), axis=0)
        span = slice(column, column + width)
        column_best[j, :, span] = jnp.maximum(column_best[j, :, span], top)

    def near(i, j):
        meet(i, j, 0, BAND, 0, HALF, False)
        meet(i, j, RB - BAND, BAND, HALF, HALF, False)

    def far(i, j):
        below = across[j, 0:1, HALF - 128 : HALF] >= down[i, BAND : BAND + 1, :]
        above = across[j, 0:1, HALF : HALF + 128] <= down[i, RB - BAND - 1 : RB - BAND, :]
        return jnp.where(below, 1.0, 0.0), jnp.where(above, 1.0, 0.0)

    def visit(first, length):
        pairs_here = [(table[0, first + u], table[1, first + u]) for u in range(length)]
        flags = [jnp.maximum(*far(i, j)) for i, j in pairs_here]
        flag = jnp.max(functools.reduce(jnp.maximum, flags))
        for i, j in pairs_here:
            near(i, j)

        @pl.when(flag > 0.0)
        def _():
            def rest(p, carry):
                i, j = table[0, p], table[1, p]
                below, above = (jnp.max(lanes) for lanes in far(i, j))

                @pl.when(below > 0.0)
                def _():
                    meet(i, j, BAND, RB - BAND, 0, HALF, False)

                @pl.when(above > 0.0)
                def _():
                    meet(i, j, 0, RB - BAND, HALF, HALF, False)

                return carry

            lax.fori_loop(first, first + length, rest, 0)

    if itself:
        meet(0, 0, 0, RB, 0, RB, True)

    def await_step(step, length):
        for u in range(length):
            block = waits[step * UNROLL + u]
            pl.when(block >= 0)(functools.partial(arrive, block))

    def some(step, carry):
        await_step(step, UNROLL)
        visit(step * UNROLL, UNROLL)
        return carry

    steps = pairs // UNROLL
    lax.fori_loop(0, steps, some, 0)
    if pairs > steps * UNROLL:
        await_step(steps, pairs - steps * UNROLL)
        visit(steps * UNROLL, pairs - steps * UNROLL)

    def found_in(k):
        found = jnp.max(column_best[k], axis=0, keepdims=True)
        if k < rows:
            turned = jnp.transpose(row_best[k])
            found = jnp.maximum(found, jnp.max(turned, axis=0, keepdims=True))
        return found

    if not lists:
        for k in range(total):
            out_ref[k : k + 1, :] = found_in(k)
        return
    for k, name in enumerate(lists[0]):
        out_ref[homes[name]] = jnp.maximum(found_in(k), found_before(name))


def meet(held, meeting, lists=(), before=()):
    rows, names = members(meeting)
    pairs = [(i, j) for i, partners in meeting for j in partners]
    itself = (0, 0) in pairs
    pairs = sorted(
        ((names.index(i), names.index(j)) for i, j in pairs if i != j), key=lambda p: p[::-1]
    )
    seen, waits = set(range(len(rows))), []
    for i, j in pairs:
        waits.append(-1 if j in seen else j)
        seen.add(j)
    total = len(names)
    shape = (128, 1, RB) if lists else (total, RB)
    in_specs = [pl.BlockSpec(memory_space=pltpu.HBM)] * total
    if lists:
        in_specs += [pl.BlockSpec(memory_space=pltpu.VMEM)] * len(before)
    return pl.pallas_call(
        functools.partial(meet_kernel, total, len(rows), pairs, itself, lists, waits),
        out_shape=jax.ShapeDtypeStruct(shape, jnp.float32),
        in_specs=in_specs,
        scratch_shapes=[
            pltpu.VMEM((total, SENT, D), jnp.bfloat16),
            pltpu.VMEM((total, 8, RB), jnp.float32),
            pltpu.VMEM((len(rows), RB, 128), jnp.float32),
            pltpu.VMEM((len(rows), RB, 128), jnp.float32),
            pltpu.VMEM((total, 8, RB), jnp.float32),
            pltpu.SMEM((2, len(pairs)), jnp.int32),
            pltpu.SMEM((len(pairs),), jnp.int32),
            pltpu.SemaphoreType.DMA((total,)),
        ],
        compiler_params=pltpu.CompilerParams(vmem_limit_bytes=66_400_000),
        cost_estimate=pl.CostEstimate(
            flops=2 * RB * RB * D * len(pairs),
            bytes_accessed=total * SENT * D * 2,
            transcendentals=0,
        ),
        name=f"meet_{len(pairs)}",
    )(
        *[held[k] for k in names],
        *before,
    )


def finish_kernel(arrived_ref, target_ref, out_ref):
    best = jnp.max(arrived_ref[...], axis=0)
    column = jnp.transpose(jnp.broadcast_to(best, (128, RB)))[:, 0:1]
    above = lax.broadcasted_iota(jnp.int32, (RB, RB), 0)
    picked = jnp.where(above == target_ref[...], column, LOW)
    out_ref[...] = jnp.max(picked, axis=0, keepdims=True)


def finish(arrived, target):
    return pl.pallas_call(
        finish_kernel, out_shape=jax.ShapeDtypeStruct((1, RB), jnp.float32), name="finish"
    )(arrived, target)


def on_device(embeds, member):
    block, target = prepare(embeds, member)
    held = {0: block}
    before = []

    def go(first):
        for i in range(first, first + 3):
            held[i] = fetch(held[PARENT[i]], (UNIT[DIRS[0][i]], UNIT[DIRS[1][i]]))

    def share(slots):
        for i in slots:
            if i + OTHER in NAMES:
                held[i + OTHER] = flip(held[i])

    def after(slots):
        for i in slots:
            before[-1], held[i] = lax.optimization_barrier((before[-1], held[i]))

    go(1)
    share((0, 1, 2, 3))
    go(4)
    before.append(meet(held, MEETINGS[0]))
    after((4, 5, 6))
    go(7)
    share((4, 5, 6))
    before.append(meet(held, MEETINGS[1]))
    after((7, 8, 9))
    go(10)
    share((7, 8, 9))
    before.append(meet(held, MEETINGS[2]))
    lists = tuple(members(meeting)[1] for meeting in (MEETINGS[-1],) + MEETINGS[:-1])
    outgoing = meet(held, MEETINGS[-1], lists, before)
    arrived = lax.all_to_all(outgoing, AXES, split_axis=0, concat_axis=0, tiled=True)
    return finish(arrived, target).reshape(-1)


def solution(mesh):
    in_specs = (P(AXES, None), P(AXES))
    return jax.shard_map(
        on_device, mesh=mesh, in_specs=in_specs, out_specs=P(AXES), check_vma=False
    )
```

```python
import functools

import jax
import jax.numpy as jnp
import numpy as np
from jax import lax
from jax.experimental import pallas as pl
from jax.experimental.pallas import tpu as pltpu
from jax.sharding import PartitionSpec as P

D = 768
RB = 512
GROUPS = 8
META = 16
SENT = RB + META
UNROLL = 4
HALF = 256
BAND = 384
ABSENT = -4.0
LOW = -1e30
AXES = ("group", "row")

UNIT = ((1, 0, 0), (0, 1, 0), (0, 0, 1), (3, 0, 0), (0, 3, 0), (0, 0, 3))
PARENT = (None,) + (0, 0, 0, 2, 1, 3, 6, 4, 4, 5, 5, 7)
DIRS = (
    (None,) + (5, 0, 2, 1, 3, 4, 0, 5, 1, 5, 2, 0),
    (None,) + (4, 3, 1, 2, 0, 5, 3, 4, 2, 4, 1, 3),
)
SLOTS = len(PARENT)
OTHER = 20
MEETINGS = (
    ((0, (0, 20)), (1, (0, 20, 21)), (2, (0, 1, 20, 21)), (3, (1, 2, 20, 21))),
    (
        (4, (0, 1, 2, 3, 21, 22)),
        (5, (2, 3, 4, 20, 21, 23, 24, 25)),
        (6, (0, 1, 4, 5, 20, 22, 23, 25, 26)),
    ),
    (
        (7, (0, 3, 4, 5, 21, 22, 23, 24, 26, 27)),
        (8, (3, 5, 6, 7, 20, 21, 24, 25, 27)),
        (9, (0, 1, 2, 5, 6, 8, 22, 26, 27)),
    ),
    ((10, (2, 9, 20, 21, 23)), (11, (2, 8, 9, 20, 26)), (12, (23, 27))),
)


def members(meeting):
    rows = tuple(k for k, partners in meeting)
    rest = sorted({k for row, partners in meeting for k in partners} - set(rows))
    return rows, rows + tuple(rest)


NAMES = tuple(sorted({k for meeting in MEETINGS for k in members(meeting)[1]}))


def offsets():
    table = []
    for core in range(2):
        held = [(0, 0, 0)]
        for i in range(1, SLOTS):
            step, base = UNIT[DIRS[core][i]], held[PARENT[i]]
            held.append(tuple((a + b) % 4 for a, b in zip(step, base)))
        table.append(held)
    return table


def place(x, y, z, core):
    group = (y // 2) * 4 + x
    row = (z * 2 + y % 2) * 2 + core
    return group * 16 + row


def fetch(block, steps):
    pairs = []
    for x in range(4):
        for y in range(4):
            for z in range(4):
                for core in range(2):
                    dx, dy, dz = steps[core]
                    source = place((x + dx) % 4, (y + dy) % 4, (z + dz) % 4, core)
                    pairs.append((source, place(x, y, z, core)))
    return lax.ppermute(block, AXES, sorted(pairs))


def flip(block):
    return lax.ppermute(block, AXES, [(i, i ^ 1) for i in range(128)])


def home(name, group, row):
    x, y, z, core = group & 3, ((group >> 2) << 1) | ((row >> 1) & 1), row >> 2, row & 1
    table = offsets()
    swap = 1 if name >= OTHER else 0
    at = []
    for axis, here in enumerate((x, y, z)):
        first = table[swap][name % OTHER][axis]
        second = table[1 - swap][name % OTHER][axis]
        at.append((here + first + core * (second - first)) & 3)
    group = ((at[1] >> 1) << 2) | at[0]
    return (group << 4) | (at[2] << 2) | ((at[1] & 1) << 1) | (core ^ swap)


def prepare_kernel(embeds_ref, member_ref, block_ref, target_ref):
    member = member_ref[...].astype(jnp.float32)
    cluster = lax.broadcasted_iota(jnp.int32, (16, RB), 0).astype(jnp.float32)
    hits = cluster == member
    ones = jnp.where(hits, 1.0, 0.0)
    above = lax.broadcasted_iota(jnp.int32, (RB, RB), 0)
    across = lax.broadcasted_iota(jnp.int32, (RB, RB), 1)
    earlier = (above < across).astype(jnp.bfloat16)
    rank = jnp.dot(ones.astype(jnp.bfloat16), earlier, preferred_element_type=jnp.float32)
    counts = jnp.sum(ones, axis=1, keepdims=True)
    parts = jnp.where(cluster < member, counts, 0.0) + jnp.where(hits, rank, 0.0)
    target = jnp.sum(parts, axis=0, keepdims=True).astype(jnp.int32)
    target_ref[...] = target
    values = embeds_ref[...].astype(jnp.float32)
    total = jnp.sum(values * values, axis=1, keepdims=True)
    normed = (values * lax.rsqrt(total + 1e-06)).astype(jnp.bfloat16)
    placer = (above == target).astype(jnp.bfloat16)
    block_ref[0:RB, :] = jnp.dot(placer, normed, preferred_element_type=jnp.float32).astype(
        jnp.bfloat16
    )
    upto = lax.broadcasted_iota(jnp.int32, (16, 16), 1) <= lax.broadcasted_iota(
        jnp.int32, (16, 16), 0
    )
    spread = jnp.transpose(jnp.broadcast_to(counts, (16, 16)))
    ends = jnp.sum(jnp.where(upto, spread, 0.0), axis=1, keepdims=True)
    places = lax.broadcasted_iota(jnp.int32, (16, RB), 1).astype(jnp.float32)
    passed = jnp.where(places >= ends, 1.0, 0.0)[0:GROUPS]
    ordered = jnp.sum(passed, axis=0, keepdims=True)
    block_ref[RB:SENT, :] = jnp.zeros((META, D), jnp.bfloat16)
    block_ref[RB:SENT, 0:RB] = jnp.broadcast_to(ordered, (META, RB)).astype(jnp.bfloat16)


def prepare(embeds, member):
    return pl.pallas_call(
        prepare_kernel,
        out_shape=(
            jax.ShapeDtypeStruct((SENT, D), jnp.bfloat16),
            jax.ShapeDtypeStruct((1, RB), jnp.int32),
        ),
        name="prepare",
    )(embeds, member.reshape(1, RB))


def meet_kernel(total, rows, pairs, itself, lists, fetched, *refs):
    blocks, refs = refs[:total], refs[total:]
    if lists:
        before, refs = refs[: len(lists) - 1], refs[len(lists) - 1 :]
    out_ref, held, across, down, row_best, column_best, table, waits, sems, *refs = refs
    for k in range(total):
        pltpu.make_async_copy(blocks[k], held.at[k], sems.at[k]).start()
    for p, (i, j) in enumerate(pairs):
        table[0, p] = i
        table[1, p] = j
        waits[p] = fetched[p]
    pairs = len(pairs)
    row_best[...] = jnp.full_like(row_best, LOW)
    column_best[...] = jnp.full_like(column_best, LOW)
    if lists:
        copies = [
            pltpu.make_async_copy(ref, found, refs[-1].at[at])
            for at, (ref, found) in enumerate(zip(before, refs[:-1]))
        ]
        before = refs[:-1]
        for copy in copies:
            copy.start()
        out_ref[...] = jnp.full_like(out_ref, ABSENT)
        here = [lax.axis_index(axis) for axis in AXES]
        homes = {name: home(name, *here) for name in NAMES}

        def found_before(name):
            found = jnp.full((1, RB), ABSENT, jnp.float32)
            for ref, names in zip(before, lists[1:]):
                if name in names:
                    at = names.index(name)
                    found = jnp.maximum(found, ref[at : at + 1, :])
            return found

        for copy in copies:
            copy.wait()
        for name in NAMES:
            if name not in lists[0]:
                out_ref[homes[name]] = found_before(name)

    def arrive(k):
        pltpu.make_async_copy(blocks[0], held.at[k], sems.at[k]).wait()
        across[k] = held[k, RB:SENT, 0:RB].astype(jnp.float32)[0:8]

    for k in range(rows):
        arrive(k)
        down[k] = jnp.transpose(jnp.broadcast_to(across[k, 0:1], (128, RB)))

    def meet(i, j, at, length, column, width, same):
        scores = lax.dot_general(
            held[i, at : at + length, :],
            held[j, column : column + width, :],
            (((1,), (1,)), ((), ())),
            preferred_element_type=jnp.float32,
        )
        here = jnp.concatenate([down[i, at : at + length, :]] * (width // 128), axis=1)
        keep = here == across[j, 0:1, column : column + width]
        if same:
            one = lax.broadcasted_iota(jnp.int32, (length, width), 0)
            keep = keep & (one != lax.broadcasted_iota(jnp.int32, (length, width), 1))
        scores = jnp.where(keep, scores, LOW)
        most = scores[:, 0:128]
        for q in range(1, width // 128):
            most = jnp.maximum(most, scores[:, 128 * q : 128 * q + 128])
        row_best[i, at : at + length, :] = jnp.maximum(row_best[i, at : at + length, :], most)
        top = jnp.max(scores.reshape(length // 8, 8, width), axis=0)
        span = slice(column, column + width)
        column_best[j, :, span] = jnp.maximum(column_best[j, :, span], top)

    def near(i, j):
        meet(i, j, 0, BAND, 0, HALF, False)
        meet(i, j, RB - BAND, BAND, HALF, HALF, False)

    def far(i, j):
        below = across[j, 0:1, HALF - 128 : HALF] >= down[i, BAND : BAND + 1, :]
        above = across[j, 0:1, HALF : HALF + 128] <= down[i, RB - BAND - 1 : RB - BAND, :]
        return jnp.where(below, 1.0, 0.0), jnp.where(above, 1.0, 0.0)

    def visit(first, length):
        pairs_here = [(table[0, first + u], table[1, first + u]) for u in range(length)]
        flags = [jnp.maximum(*far(i, j)) for i, j in pairs_here]
        flag = jnp.max(functools.reduce(jnp.maximum, flags))
        for i, j in pairs_here:
            near(i, j)

        @pl.when(flag > 0.0)
        def _():
            def rest(p, carry):
                i, j = table[0, p], table[1, p]
                below, above = (jnp.max(lanes) for lanes in far(i, j))

                @pl.when(below > 0.0)
                def _():
                    meet(i, j, BAND, RB - BAND, 0, HALF, False)

                @pl.when(above > 0.0)
                def _():
                    meet(i, j, 0, RB - BAND, HALF, HALF, False)

                return carry

            lax.fori_loop(first, first + length, rest, 0)

    if itself:
        meet(0, 0, 0, RB, 0, RB, True)

    def await_step(step, length):
        for u in range(length):
            block = waits[step * UNROLL + u]
            pl.when(block >= 0)(functools.partial(arrive, block))

    def some(step, carry):
        await_step(step, UNROLL)
        visit(step * UNROLL, UNROLL)
        return carry

    steps = pairs // UNROLL
    lax.fori_loop(0, steps, some, 0)
    if pairs > steps * UNROLL:
        await_step(steps, pairs - steps * UNROLL)
        visit(steps * UNROLL, pairs - steps * UNROLL)

    def found_in(k):
        found = jnp.max(column_best[k], axis=0, keepdims=True)
        if k < rows:
            turned = jnp.transpose(row_best[k])
            found = jnp.maximum(found, jnp.max(turned, axis=0, keepdims=True))
        return found

    if not lists:
        for k in range(total):
            out_ref[k : k + 1, :] = found_in(k)
        return
    for k, name in enumerate(lists[0]):
        out_ref[homes[name]] = jnp.maximum(found_in(k), found_before(name))


def meet(held, meeting, lists=(), before=()):
    rows, names = members(meeting)
    pairs = [(i, j) for i, partners in meeting for j in partners]
    itself = (0, 0) in pairs
    pairs = sorted(
        ((names.index(i), names.index(j)) for i, j in pairs if i != j), key=lambda p: p[::-1]
    )
    seen, waits = set(range(len(rows))), []
    for i, j in pairs:
        waits.append(-1 if j in seen else j)
        seen.add(j)
    total = len(names)
    shape = (128, 1, RB) if lists else (total, RB)
    in_specs = [pl.BlockSpec(memory_space=pltpu.HBM)] * total
    if lists:
        in_specs += [pl.BlockSpec(memory_space=pltpu.HBM)] * len(before)
    return pl.pallas_call(
        functools.partial(meet_kernel, total, len(rows), pairs, itself, lists, waits),
        out_shape=jax.ShapeDtypeStruct(shape, jnp.float32),
        in_specs=in_specs,
        scratch_shapes=[
            pltpu.VMEM((total, SENT, D), jnp.bfloat16),
            pltpu.VMEM((total, 8, RB), jnp.float32),
            pltpu.VMEM((len(rows), RB, 128), jnp.float32),
            pltpu.VMEM((len(rows), RB, 128), jnp.float32),
            pltpu.VMEM((total, 8, RB), jnp.float32),
            pltpu.SMEM((2, len(pairs)), jnp.int32),
            pltpu.SMEM((len(pairs),), jnp.int32),
            pltpu.SemaphoreType.DMA((total,)),
        ]
        + [pltpu.VMEM(ref.shape, jnp.float32) for ref in before]
        + ([pltpu.SemaphoreType.DMA((len(before),))] if lists else []),
        compiler_params=pltpu.CompilerParams(vmem_limit_bytes=66_400_000),
        cost_estimate=pl.CostEstimate(
            flops=2 * RB * RB * D * len(pairs),
            bytes_accessed=total * SENT * D * 2,
            transcendentals=0,
        ),
        name=f"meet_{len(pairs)}",
    )(
        *[held[k] for k in names],
        *before,
    )


def finish_kernel(arrived_ref, target_ref, out_ref):
    best = jnp.max(arrived_ref[...], axis=0)
    column = jnp.transpose(jnp.broadcast_to(best, (128, RB)))[:, 0:1]
    above = lax.broadcasted_iota(jnp.int32, (RB, RB), 0)
    picked = jnp.where(above == target_ref[...], column, LOW)
    out_ref[...] = jnp.max(picked, axis=0, keepdims=True)


def finish(arrived, target):
    return pl.pallas_call(
        finish_kernel, out_shape=jax.ShapeDtypeStruct((1, RB), jnp.float32), name="finish"
    )(arrived, target)


def on_device(embeds, member):
    block, target = prepare(embeds, member)
    held = {0: block}
    before = []

    def go(first):
        for i in range(first, first + 3):
            held[i] = fetch(held[PARENT[i]], (UNIT[DIRS[0][i]], UNIT[DIRS[1][i]]))

    def share(slots):
        for i in slots:
            if i + OTHER in NAMES:
                held[i + OTHER] = flip(held[i])

    def after(slots):
        for i in slots:
            before[-1], held[i] = lax.optimization_barrier((before[-1], held[i]))

    go(1)
    share((0, 1, 2, 3))
    go(4)
    before.append(meet(held, MEETINGS[0]))
    after((4, 5, 6))
    go(7)
    share((4, 5, 6))
    before.append(meet(held, MEETINGS[1]))
    after((7, 8, 9))
    go(10)
    share((7, 8, 9))
    before.append(meet(held, MEETINGS[2]))
    lists = tuple(members(meeting)[1] for meeting in (MEETINGS[-1],) + MEETINGS[:-1])
    outgoing = meet(held, MEETINGS[-1], lists, before)
    arrived = lax.all_to_all(outgoing, AXES, split_axis=0, concat_axis=0, tiled=True)
    return finish(arrived, target).reshape(-1)


def solution(mesh):
    in_specs = (P(AXES, None), P(AXES))
    return jax.shard_map(
        on_device, mesh=mesh, in_specs=in_specs, out_specs=P(AXES), check_vma=False
    )
```

```python
import functools

import jax
import jax.numpy as jnp
import numpy as np
from jax import lax
from jax.experimental import pallas as pl
from jax.experimental.pallas import tpu as pltpu
from jax.sharding import PartitionSpec as P

D = 768
RB = 512
GROUPS = 8
META = 16
SENT = RB + META
UNROLL = 7
HALF = 256
BAND = 384
ABSENT = -4.0
LOW = -1e30
AXES = ("group", "row")

UNIT = ((1, 0, 0), (0, 1, 0), (0, 0, 1), (3, 0, 0), (0, 3, 0), (0, 0, 3))
PARENT = (None,) + (0, 0, 0, 2, 1, 3, 6, 4, 4, 5, 5, 7)
DIRS = (
    (None,) + (5, 0, 2, 1, 3, 4, 0, 5, 1, 5, 2, 0),
    (None,) + (4, 3, 1, 2, 0, 5, 3, 4, 2, 4, 1, 3),
)
SLOTS = len(PARENT)
OTHER = 20
MEETINGS = (
    ((0, (0, 20)), (1, (0, 20, 21)), (2, (0, 1, 20, 21)), (3, (1, 2, 20, 21))),
    (
        (4, (0, 1, 2, 3, 21, 22)),
        (5, (2, 3, 4, 20, 21, 23, 24, 25)),
        (6, (0, 1, 4, 5, 20, 22, 23, 25, 26)),
    ),
    (
        (7, (0, 3, 4, 5, 21, 22, 23, 24, 26, 27)),
        (8, (3, 5, 6, 7, 20, 21, 24, 25, 27)),
        (9, (0, 1, 2, 5, 6, 8, 22, 26, 27)),
    ),
    ((10, (2, 9, 20, 21, 23)), (11, (2, 8, 9, 20, 26)), (12, (23, 27))),
)


def members(meeting):
    rows = tuple(k for k, partners in meeting)
    rest = sorted({k for row, partners in meeting for k in partners} - set(rows))
    return rows, rows + tuple(rest)


NAMES = tuple(sorted({k for meeting in MEETINGS for k in members(meeting)[1]}))


def offsets():
    table = []
    for core in range(2):
        held = [(0, 0, 0)]
        for i in range(1, SLOTS):
            step, base = UNIT[DIRS[core][i]], held[PARENT[i]]
            held.append(tuple((a + b) % 4 for a, b in zip(step, base)))
        table.append(held)
    return table


def place(x, y, z, core):
    group = (y // 2) * 4 + x
    row = (z * 2 + y % 2) * 2 + core
    return group * 16 + row


def fetch(block, steps):
    pairs = []
    for x in range(4):
        for y in range(4):
            for z in range(4):
                for core in range(2):
                    dx, dy, dz = steps[core]
                    source = place((x + dx) % 4, (y + dy) % 4, (z + dz) % 4, core)
                    pairs.append((source, place(x, y, z, core)))
    return lax.ppermute(block, AXES, sorted(pairs))


def flip(block):
    return lax.ppermute(block, AXES, [(i, i ^ 1) for i in range(128)])


def home(name, group, row):
    x, y, z, core = group & 3, ((group >> 2) << 1) | ((row >> 1) & 1), row >> 2, row & 1
    table = offsets()
    swap = 1 if name >= OTHER else 0
    at = []
    for axis, here in enumerate((x, y, z)):
        first = table[swap][name % OTHER][axis]
        second = table[1 - swap][name % OTHER][axis]
        at.append((here + first + core * (second - first)) & 3)
    group = ((at[1] >> 1) << 2) | at[0]
    return (group << 4) | (at[2] << 2) | ((at[1] & 1) << 1) | (core ^ swap)


def prepare_kernel(embeds_ref, member_ref, block_ref, target_ref):
    member = member_ref[...].astype(jnp.float32)
    cluster = lax.broadcasted_iota(jnp.int32, (16, RB), 0).astype(jnp.float32)
    hits = cluster == member
    ones = jnp.where(hits, 1.0, 0.0)
    above = lax.broadcasted_iota(jnp.int32, (RB, RB), 0)
    across = lax.broadcasted_iota(jnp.int32, (RB, RB), 1)
    earlier = (above < across).astype(jnp.bfloat16)
    rank = jnp.dot(ones.astype(jnp.bfloat16), earlier, preferred_element_type=jnp.float32)
    counts = jnp.sum(ones, axis=1, keepdims=True)
    parts = jnp.where(cluster < member, counts, 0.0) + jnp.where(hits, rank, 0.0)
    target = jnp.sum(parts, axis=0, keepdims=True).astype(jnp.int32)
    target_ref[...] = target
    values = embeds_ref[...].astype(jnp.float32)
    total = jnp.sum(values * values, axis=1, keepdims=True)
    normed = (values * lax.rsqrt(total + 1e-06)).astype(jnp.bfloat16)
    placer = (above == target).astype(jnp.bfloat16)
    block_ref[0:RB, :] = jnp.dot(placer, normed, preferred_element_type=jnp.float32).astype(
        jnp.bfloat16
    )
    upto = lax.broadcasted_iota(jnp.int32, (16, 16), 1) <= lax.broadcasted_iota(
        jnp.int32, (16, 16), 0
    )
    spread = jnp.transpose(jnp.broadcast_to(counts, (16, 16)))
    ends = jnp.sum(jnp.where(upto, spread, 0.0), axis=1, keepdims=True)
    places = lax.broadcasted_iota(jnp.int32, (16, RB), 1).astype(jnp.float32)
    passed = jnp.where(places >= ends, 1.0, 0.0)[0:GROUPS]
    ordered = jnp.sum(passed, axis=0, keepdims=True)
    block_ref[RB:SENT, :] = jnp.zeros((META, D), jnp.bfloat16)
    block_ref[RB:SENT, 0:RB] = jnp.broadcast_to(ordered, (META, RB)).astype(jnp.bfloat16)


def prepare(embeds, member):
    return pl.pallas_call(
        prepare_kernel,
        out_shape=(
            jax.ShapeDtypeStruct((SENT, D), jnp.bfloat16),
            jax.ShapeDtypeStruct((1, RB), jnp.int32),
        ),
        name="prepare",
    )(embeds, member.reshape(1, RB))


def meet_kernel(total, rows, pairs, itself, lists, fetched, *refs):
    blocks, refs = refs[:total], refs[total:]
    if lists:
        before, refs = refs[: len(lists) - 1], refs[len(lists) - 1 :]
    out_ref, held, across, down, row_best, column_best, table, waits, sems = refs
    for k in range(total):
        pltpu.make_async_copy(blocks[k], held.at[k], sems.at[k]).start()
    for p, (i, j) in enumerate(pairs):
        table[0, p] = i
        table[1, p] = j
        waits[p] = fetched[p]
    pairs = len(pairs)
    row_best[...] = jnp.full_like(row_best, LOW)
    column_best[...] = jnp.full_like(column_best, LOW)
    if lists:
        out_ref[...] = jnp.full_like(out_ref, ABSENT)
        here = [lax.axis_index(axis) for axis in AXES]
        homes = {name: home(name, *here) for name in NAMES}

        def found_before(name):
            found = jnp.full((1, RB), ABSENT, jnp.float32)
            for ref, names in zip(before, lists[1:]):
                if name in names:
                    at = names.index(name)
                    found = jnp.maximum(found, ref[at : at + 1, :])
            return found

        for name in NAMES:
            if name not in lists[0]:
                out_ref[homes[name]] = found_before(name)

    def arrive(k):
        pltpu.make_async_copy(blocks[0], held.at[k], sems.at[k]).wait()
        across[k] = held[k, RB:SENT, 0:RB].astype(jnp.float32)[0:8]

    for k in range(rows):
        arrive(k)
        down[k] = jnp.transpose(jnp.broadcast_to(across[k, 0:1], (128, RB)))

    def meet(i, j, at, length, column, width, same):
        scores = lax.dot_general(
            held[i, at : at + length, :],
            held[j, column : column + width, :],
            (((1,), (1,)), ((), ())),
            preferred_element_type=jnp.float32,
        )
        here = jnp.concatenate([down[i, at : at + length, :]] * (width // 128), axis=1)
        keep = here == across[j, 0:1, column : column + width]
        if same:
            one = lax.broadcasted_iota(jnp.int32, (length, width), 0)
            keep = keep & (one != lax.broadcasted_iota(jnp.int32, (length, width), 1))
        scores = jnp.where(keep, scores, LOW)
        most = scores[:, 0:128]
        for q in range(1, width // 128):
            most = jnp.maximum(most, scores[:, 128 * q : 128 * q + 128])
        row_best[i, at : at + length, :] = jnp.maximum(row_best[i, at : at + length, :], most)
        top = jnp.max(scores.reshape(length // 8, 8, width), axis=0)
        span = slice(column, column + width)
        column_best[j, :, span] = jnp.maximum(column_best[j, :, span], top)

    def near(i, j):
        meet(i, j, 0, BAND, 0, HALF, False)
        meet(i, j, RB - BAND, BAND, HALF, HALF, False)

    def far(i, j):
        below = across[j, 0:1, HALF - 128 : HALF] >= down[i, BAND : BAND + 1, :]
        above = across[j, 0:1, HALF : HALF + 128] <= down[i, RB - BAND - 1 : RB - BAND, :]
        return jnp.where(below, 1.0, 0.0), jnp.where(above, 1.0, 0.0)

    def visit(first, length):
        pairs_here = [(table[0, first + u], table[1, first + u]) for u in range(length)]
        flags = [jnp.maximum(*far(i, j)) for i, j in pairs_here]
        flag = jnp.max(functools.reduce(jnp.maximum, flags))
        for i, j in pairs_here:
            near(i, j)

        @pl.when(flag > 0.0)
        def _():
            def rest(p, carry):
                i, j = table[0, p], table[1, p]
                below, above = (jnp.max(lanes) for lanes in far(i, j))

                @pl.when(below > 0.0)
                def _():
                    meet(i, j, BAND, RB - BAND, 0, HALF, False)

                @pl.when(above > 0.0)
                def _():
                    meet(i, j, 0, RB - BAND, HALF, HALF, False)

                return carry

            lax.fori_loop(first, first + length, rest, 0)

    if itself:
        meet(0, 0, 0, RB, 0, RB, True)

    def await_step(step, length):
        for u in range(length):
            block = waits[step * UNROLL + u]
            pl.when(block >= 0)(functools.partial(arrive, block))

    def some(step, carry):
        await_step(step, UNROLL)
        visit(step * UNROLL, UNROLL)
        return carry

    steps = pairs // UNROLL
    lax.fori_loop(0, steps, some, 0)
    if pairs > steps * UNROLL:
        await_step(steps, pairs - steps * UNROLL)
        visit(steps * UNROLL, pairs - steps * UNROLL)

    def found_in(k):
        found = jnp.max(column_best[k], axis=0, keepdims=True)
        if k < rows:
            turned = jnp.transpose(row_best[k])
            found = jnp.maximum(found, jnp.max(turned, axis=0, keepdims=True))
        return found

    if not lists:
        for k in range(total):
            out_ref[k : k + 1, :] = found_in(k)
        return
    for k, name in enumerate(lists[0]):
        out_ref[homes[name]] = jnp.maximum(found_in(k), found_before(name))


def meet(held, meeting, lists=(), before=()):
    rows, names = members(meeting)
    pairs = [(i, j) for i, partners in meeting for j in partners]
    itself = (0, 0) in pairs
    pairs = sorted(
        ((names.index(i), names.index(j)) for i, j in pairs if i != j), key=lambda p: p[::-1]
    )
    seen, waits = set(range(len(rows))), []
    for i, j in pairs:
        waits.append(-1 if j in seen else j)
        seen.add(j)
    total = len(names)
    shape = (128, 1, RB) if lists else (total, RB)
    in_specs = [pl.BlockSpec(memory_space=pltpu.HBM)] * total
    if lists:
        in_specs += [pl.BlockSpec(memory_space=pltpu.VMEM)] * len(before)
    return pl.pallas_call(
        functools.partial(meet_kernel, total, len(rows), pairs, itself, lists, waits),
        out_shape=jax.ShapeDtypeStruct(shape, jnp.float32),
        in_specs=in_specs,
        scratch_shapes=[
            pltpu.VMEM((total, SENT, D), jnp.bfloat16),
            pltpu.VMEM((total, 8, RB), jnp.float32),
            pltpu.VMEM((len(rows), RB, 128), jnp.float32),
            pltpu.VMEM((len(rows), RB, 128), jnp.float32),
            pltpu.VMEM((total, 8, RB), jnp.float32),
            pltpu.SMEM((2, len(pairs)), jnp.int32),
            pltpu.SMEM((len(pairs),), jnp.int32),
            pltpu.SemaphoreType.DMA((total,)),
        ],
        compiler_params=pltpu.CompilerParams(vmem_limit_bytes=66_400_000),
        cost_estimate=pl.CostEstimate(
            flops=2 * RB * RB * D * len(pairs),
            bytes_accessed=total * SENT * D * 2,
            transcendentals=0,
        ),
        name=f"meet_{len(pairs)}",
    )(
        *[held[k] for k in names],
        *before,
    )


def finish_kernel(arrived_ref, target_ref, out_ref):
    best = jnp.max(arrived_ref[...], axis=0)
    column = jnp.transpose(jnp.broadcast_to(best, (128, RB)))[:, 0:1]
    above = lax.broadcasted_iota(jnp.int32, (RB, RB), 0)
    picked = jnp.where(above == target_ref[...], column, LOW)
    out_ref[...] = jnp.max(picked, axis=0, keepdims=True)


def finish(arrived, target):
    return pl.pallas_call(
        finish_kernel, out_shape=jax.ShapeDtypeStruct((1, RB), jnp.float32), name="finish"
    )(arrived, target)


def on_device(embeds, member):
    block, target = prepare(embeds, member)
    held = {0: block}
    before = []

    def go(first):
        for i in range(first, first + 3):
            held[i] = fetch(held[PARENT[i]], (UNIT[DIRS[0][i]], UNIT[DIRS[1][i]]))

    def share(slots):
        for i in slots:
            if i + OTHER in NAMES:
                held[i + OTHER] = flip(held[i])

    def after(slots):
        for i in slots:
            before[-1], held[i] = lax.optimization_barrier((before[-1], held[i]))

    go(1)
    share((0, 1, 2, 3))
    go(4)
    before.append(meet(held, MEETINGS[0]))
    after((4, 5, 6))
    go(7)
    share((4, 5, 6))
    before.append(meet(held, MEETINGS[1]))
    after((7, 8, 9))
    go(10)
    share((7, 8, 9))
    before.append(meet(held, MEETINGS[2]))
    lists = tuple(members(meeting)[1] for meeting in (MEETINGS[-1],) + MEETINGS[:-1])
    outgoing = meet(held, MEETINGS[-1], lists, before)
    arrived = lax.all_to_all(outgoing, AXES, split_axis=0, concat_axis=0, tiled=True)
    return finish(arrived, target).reshape(-1)


def solution(mesh):
    in_specs = (P(AXES, None), P(AXES))
    return jax.shard_map(
        on_device, mesh=mesh, in_specs=in_specs, out_specs=P(AXES), check_vma=False
    )
```
